512 devices in a mesh: dp: 16 (over z_lo, core), code: 32 (over z_hi, y, x).
Axes of the slice: x: 4, y: 4, z: 16 (z_hi: 2, z_lo: 8; z = z_hi * 8 + z_lo), core: 2. Of those that a mesh axis runs over, the one named last changes fastest.
Arguments:
- latents: bfloat16 [16384, 256], P('dp'), may hold values from -30 to 30
- codebook: bfloat16 [131072, 256], P('code'), may hold values from -6 to 6
- old_counts: float32 [131072], P('code'), may hold values from 0.002 to 0.02
- old_sums: float32 [256, 131072], P('dp', 'code'), may hold values from -0.06 to 0.06
Outputs:
- quantized: bfloat16 [16384, 256], P('dp')
- counts_next: float32 [131072], P('code')
- codebook_next: float32 [256, 131072], P('dp', 'code')
The draws below stay inside these ranges and needn't reach their ends.
All inputs are finite; a program needn't handle non-finite values.
Results may differ from the reference program's by a relative error of at most 0.0043.
Values may be sent and summed in bfloat16 or wider, within the bound.
A program may use at most 64 MiB of HBM per device.

```python
import math
import jax
import jax.numpy as jnp
from jax import lax

D = 256
CODES = 131072
ROWS = 16384


def pair_codes(key):
    seed_key = jax.random.fold_in(key, 101)
    base_key = jax.random.fold_in(seed_key, 0)
    base_codes = jnp.clip(jax.random.normal(base_key, (CODES, D), jnp.float32), -6.0, 6.0)
    pair_count = CODES // 2
    paired = base_codes.reshape(pair_count, 2, D)
    mixed = paired
    return mixed.reshape(CODES, D)


def draw_codebook(key, part):
    codes_all = pair_codes(key)
    return codes_all.astype(jnp.bfloat16)


def draw_latents(key, part):
    own_key = jax.random.fold_in(key, 7)
    rows_key = jax.random.fold_in(own_key, 0)
    rows_all = jnp.clip(jax.random.normal(rows_key, (ROWS, D), jnp.float32), -6.0, 6.0)
    return rows_all.astype(jnp.bfloat16)


def shard_levels(key, dims, pieces, least, top_value):
    level = 1.0
    for position, blocks in pieces:
        steps = jax.random.uniform(jax.random.fold_in(jax.random.fold_in(key, 6), position), (blocks,), jnp.float32, least / len(pieces), top_value / len(pieces))
        level = level * jnp.repeat(jnp.exp(steps), dims[position] // blocks).reshape((-1,) + (1,) * (len(dims) - 1 - position))
    return level


def gaussian(rng, dims, spread, limit, cuts=(), held_as=jnp.bfloat16):
    result = jax.random.normal(rng, dims, jnp.float32) * spread
    if len(cuts) > 0:
        result = shard_levels(rng, dims, cuts, -0.22, 0.18) * result
    return jnp.clip(result, min=-limit, max=limit).astype(held_as)


def setup_inputs(seed: int = 0) -> dict:
    arg_keys = jax.random.split(jax.random.key(seed), 5)
    latents = draw_latents(jax.random.fold_in(arg_keys[4], 71), 0)
    codebook = draw_codebook(jax.random.fold_in(arg_keys[4], 71), 0)
    old_counts = jnp.clip(jnp.exp(math.log(0.02) - 2.30258502 * jax.random.uniform(arg_keys[2], (CODES,), jnp.float32) ** shard_levels(arg_keys[2], (CODES,), ((0, 32),), -0.2, 0.2)), 0.002, 0.02)
    old_sums = gaussian(arg_keys[3], (D, CODES), 0.01, 0.06, ((0, 16), (1, 32)), jnp.float32)
    return dict(latents=latents, codebook=codebook, old_counts=old_counts, old_sums=old_sums)


def reference(latents, codebook, old_counts, old_sums):
    logit_scale = 2.0 / math.sqrt(D)
    code_norms = lax.optimization_barrier(jnp.sum(jnp.square(codebook.astype(jnp.float32)), axis=1))
    block_rows = min(512, ROWS)
    row_blocks = latents.reshape(ROWS // block_rows, block_rows, D)

    def advance(running, row_block):
        counts, code_sums = running
        logits = (2.0 * jnp.dot(row_block, codebook.T, preferred_element_type=jnp.float32) - code_norms[None, :]) * logit_scale
        row_top = lax.optimization_barrier(jnp.max(logits, axis=1, keepdims=True))
        raised = jnp.exp(logits - row_top)
        row_total = lax.optimization_barrier(jnp.sum(raised, axis=1, keepdims=True))
        weights = (raised / row_total).astype(jnp.bfloat16)
        quant_rows = jnp.dot(weights, codebook, preferred_element_type=jnp.float32).astype(jnp.bfloat16)
        counts = counts + lax.optimization_barrier(jnp.sum(weights.astype(jnp.float32), axis=0))
        code_sums = code_sums + jnp.dot(row_block.T, weights, preferred_element_type=jnp.float32)
        return ((counts, code_sums), quant_rows)
    start_pair = (jnp.zeros((CODES,), jnp.float32), jnp.zeros((D, CODES), jnp.float32))
    (counts, code_sums), quant_blocks = lax.scan(advance, start_pair, row_blocks)
    quantized = quant_blocks.reshape(ROWS, D)
    counts_next = 0.9 * old_counts + 0.1 * counts
    sums_next = 0.9 * old_sums + 0.1 * code_sums
    codebook_next = sums_next / counts_next[None, :]
    return (quantized, counts_next, codebook_next)
```

```python
import math

import jax
import jax.numpy as jnp
from jax import lax
from jax.experimental import pallas as pl
from jax.experimental.pallas import tpu as pltpu
from jax.sharding import PartitionSpec as P

MESH = pl.DeviceIdType.MESH
F32 = jnp.float32
BF16 = jnp.bfloat16

ROWS = 1024
CODES = 4096
WIDTH = 256
BLOCK = 512
BLOCKS = CODES // BLOCK
PLANE = 16
PIECE = WIDTH // PLANE
LINE = 8
SUBS = 4
SUB = CODES // SUBS
SHARE = 16
HALF = SHARE * LINE


def dot(a, b):
    return lax.dot_general(a, b, (((1,), (0,)), ((), ())), preferred_element_type=F32)


def dot_t(a, b):
    return lax.dot_general(a, b, (((1,), (1,)), ((), ())), preferred_element_type=F32)


def kernel(
    latents_hbm, codebook_hbm, old_counts_ref, old_sums_ref,
    quant_ref, counts_ref, next_ref,
    lat, lat_t, code, code_t, logits, raised,
    stat_in, zstat_out, zstat_in,
    q_acc, q_send, q_in, zq_out, zq_in, q_all,
    scaled, own, pair_out, pair_in, cnt, cnt_pair, cnt_right, cnt_left, cnt_to_right, cnt_to_left,
    right_in, left_in, right_out, left_out,
    lat_sem, code_sem,
    stat_s, stat_r, zstat_sem, q_s, q_r, zq_sem, qa_s, qa_r,
    pair_s, pair_r, cntp_sem, cntr_sem, cntl_sem, right_s, right_r, left_s, left_r,
):
    dp = lax.axis_index("dp")
    cd = lax.axis_index("code")
    z = dp // 2
    core = dp % 2
    zh = cd // PLANE
    xy = cd % PLANE
    partner = (dp + 1 - 2 * core, cd)
    across = (dp, (1 - zh) * PLANE + xy)

    def peer(i):
        j = (xy + i) % PLANE
        return j, (dp, zh * PLANE + j)

    lat_copy = pltpu.make_async_copy(latents_hbm, lat, lat_sem)
    lat_copy.start()

    def code_copy(b):
        rows = pl.ds(pl.multiple_of(b * BLOCK, BLOCK), BLOCK)
        return pltpu.make_async_copy(codebook_hbm.at[rows], code.at[rows], code_sem.at[b])

    for b in range(BLOCKS):
        code_copy(b).start()

    barrier = pltpu.get_barrier_semaphore()

    def greet(i, carry):
        pl.semaphore_signal(barrier, inc=1, device_id=peer(i)[1], device_id_type=MESH)
        return carry

    lax.fori_loop(1, PLANE, greet, 0)
    pl.semaphore_signal(barrier, inc=1, device_id=partner, device_id_type=MESH)
    pl.semaphore_signal(barrier, inc=1, device_id=across, device_id_type=MESH)

    @pl.when(z > 0)
    def _():
        pl.semaphore_signal(barrier, inc=1, device_id=(dp - 2, cd), device_id_type=MESH)

    @pl.when(z < LINE - 1)
    def _():
        pl.semaphore_signal(barrier, inc=1, device_id=(dp + 2, cd), device_id_type=MESH)

    lat_copy.wait()
    lat_t[...] = lat[...].T

    per_dot = 2.0 * 2.0 / math.sqrt(WIDTH) * math.log2(math.e)
    per_norm = 2.0 / math.sqrt(WIDTH) * math.log2(math.e)

    def first(b, top):
        code_copy(b).wait()
        rows = pl.ds(pl.multiple_of(b * BLOCK, BLOCK), BLOCK)
        block = code[rows, :]
        wide = block.astype(F32)
        norms = jnp.sum(wide * wide, axis=1, keepdims=True) * per_norm
        part = dot(block, lat_t[...]) * per_dot - norms
        logits[rows, :] = part
        code_t[:, rows] = block.T
        return jnp.maximum(top, jnp.max(part.reshape(BLOCK // 8, 8, ROWS), axis=0))

    top = lax.fori_loop(0, BLOCKS, first, jnp.full((8, ROWS), -jnp.inf, F32))
    top = jnp.max(top, axis=0, keepdims=True)

    q_acc[...] = jnp.zeros_like(q_acc)

    def second(b, total):
        rows = pl.ds(pl.multiple_of(b * BLOCK, BLOCK), BLOCK)
        part = jnp.exp2(logits[rows, :] - top)
        low = part.astype(BF16)
        raised[rows, :] = low
        q_acc[...] += dot(code_t[:, rows], low)
        return total + jnp.sum(part.reshape(BLOCK // 8, 8, ROWS), axis=0)

    total = lax.fori_loop(0, BLOCKS, second, jnp.zeros((8, ROWS), F32))
    total = jnp.sum(total, axis=0, keepdims=True)

    stat_in[xy, 0:1, :] = top
    stat_in[xy, 1:2, :] = total
    ends = (z == 0) | (z == LINE - 1)

    @pl.when(ends)
    def _():
        pl.semaphore_wait(barrier, PLANE + 2)

    @pl.when(jnp.logical_not(ends))
    def _():
        pl.semaphore_wait(barrier, PLANE + 3)

    def stat_copy(i):
        j, device = peer(i)
        return pltpu.make_async_remote_copy(
            stat_in.at[xy], stat_in.at[xy], stat_s.at[i], stat_r.at[xy], device_id=device, device_id_type=MESH)

    def stat_wait(i):
        j, device = peer(i)
        pltpu.make_async_remote_copy(
            stat_in.at[j], stat_in.at[j], stat_s.at[i], stat_r.at[j], device_id=device, device_id_type=MESH).wait_recv()

    def each(run):
        def step(i, carry):
            run(i)
            return carry
        lax.fori_loop(1, PLANE, step, 0)

    each(lambda i: stat_copy(i).start())

    q_send[...] = q_acc[...].astype(BF16)

    def piece(j):
        return pl.ds(pl.multiple_of(j * PIECE, PIECE), PIECE)

    def q_copy(i):
        j, device = peer(i)
        return pltpu.make_async_remote_copy(
            q_send.at[piece(j)], q_in.at[xy], q_s.at[i], q_r.at[xy], device_id=device, device_id_type=MESH)

    def q_wait(i):
        j, device = peer(i)
        pltpu.make_async_remote_copy(
            q_send.at[piece(j)], q_in.at[j], q_s.at[i], q_r.at[j], device_id=device, device_id_type=MESH).wait_recv()

    each(lambda i: q_copy(i).start())
    q_in[xy] = q_send[piece(xy), :]

    each(stat_wait)
    plane_top = stat_in[0, 0:1, :]
    for j in range(1, PLANE):
        plane_top = jnp.maximum(plane_top, stat_in[j, 0:1, :])
    plane_total = jnp.zeros((1, ROWS), F32)
    for j in range(PLANE):
        plane_total += stat_in[j, 1:2, :] * jnp.exp2(stat_in[j, 0:1, :] - plane_top)
    zstat_out[0:1, :] = plane_top
    zstat_out[1:2, :] = plane_total
    zstat_copy = pltpu.make_async_remote_copy(
        zstat_out, zstat_in, zstat_sem.at[0], zstat_sem.at[1], device_id=across, device_id_type=MESH)
    zstat_copy.start()

    each(q_wait)
    plane_q = jnp.zeros((PIECE, ROWS), F32)
    for j in range(PLANE):
        plane_q += q_in[j].astype(F32) * jnp.exp2(stat_in[j, 0:1, :] - plane_top)
    zq_out[...] = plane_q.astype(BF16)
    zq_copy = pltpu.make_async_remote_copy(
        zq_out, zq_in, zq_sem.at[0], zq_sem.at[1], device_id=across, device_id_type=MESH)
    zq_copy.start()

    zstat_copy.wait_recv()
    other_top = zstat_in[0:1, :]
    full_top = jnp.maximum(plane_top, other_top)
    mine_factor = jnp.exp2(plane_top - full_top)
    other_factor = jnp.exp2(other_top - full_top)
    full_total = plane_total * mine_factor + zstat_in[1:2, :] * other_factor
    inverse = 1.0 / full_total
    factor = jnp.exp2(top - full_top) * inverse

    for side in range(2):
        which = core if side == 0 else 1 - core
        for c in range(LINE):
            src = pl.ds(pl.multiple_of(c * 2 * SHARE + which * SHARE, SHARE), SHARE)
            scaled[side * HALF + c * SHARE : side * HALF + (c + 1) * SHARE, :] = (
                lat_t[src, :].astype(F32) * factor).astype(BF16)
    high = factor.astype(BF16)
    rest = (factor - high.astype(F32)).astype(BF16)
    line_no = lax.broadcasted_iota(jnp.int32, (SHARE, ROWS), 0)
    scaled[WIDTH : WIDTH + SHARE, :] = jnp.where(
        line_no == 0, high.astype(F32), jnp.where(line_no == 1, rest.astype(F32), 0.0)).astype(BF16)

    def sub(q):
        return pl.ds(q * SUB, SUB)

    def pair_copy(q):
        return pltpu.make_async_remote_copy(
            pair_out.at[:, sub(q)], pair_in.at[:, sub(q)], pair_s.at[q], pair_r.at[q],
            device_id=partner, device_id_type=MESH)

    for q in range(SUBS):
        sums = dot_t(scaled[...], raised[sub(q), :])
        pair_out[:, sub(q)] = sums[HALF:WIDTH].astype(BF16)
        pair_copy(q).start()
        own[:, sub(q)] = sums[0:HALF]
        cnt[:, sub(q)] = sums[WIDTH : WIDTH + 1] + sums[WIDTH + 1 : WIDTH + 2]

    cntp_copy = pltpu.make_async_remote_copy(
        cnt, cnt_pair, cntp_sem.at[0], cntp_sem.at[1], device_id=partner, device_id_type=MESH)
    cntp_copy.start()

    def right_copy(t, q):
        return pltpu.make_async_remote_copy(
            right_out.at[t, :, sub(q)], right_in.at[t, :, sub(q)], right_s.at[t, q], right_r.at[t, q],
            device_id=(dp + 2, cd), device_id_type=MESH)

    def left_copy(t, q):
        return pltpu.make_async_remote_copy(
            left_out.at[t, :, sub(q)], left_in.at[t, :, sub(q)], left_s.at[t, q], left_r.at[t, q],
            device_id=(dp - 2, cd), device_id_type=MESH)

    def share(c):
        return pl.ds(pl.multiple_of(c * SHARE, SHARE), SHARE)

    last = LINE - 1

    def right_step(t, q):
        @pl.when(t >= z)
        def _():
            mine = own[share(last - t + z), sub(q)]
            if t == 0:
                right_out[t, :, sub(q)] = mine.astype(BF16)
            else:
                @pl.when(z > 0)
                def _():
                    right_copy(t - 1, q).wait_recv()
                    right_out[t, :, sub(q)] = (mine + right_in[t - 1, :, sub(q)].astype(F32)).astype(BF16)

                @pl.when(z == 0)
                def _():
                    right_out[t, :, sub(q)] = mine.astype(BF16)
            right_copy(t, q).start()

    def left_step(t, q):
        @pl.when(t >= last - z)
        def _():
            mine = own[share(t - last + z), sub(q)]
            if t == 0:
                left_out[t, :, sub(q)] = mine.astype(BF16)
            else:
                @pl.when(z < last)
                def _():
                    left_copy(t - 1, q).wait_recv()
                    left_out[t, :, sub(q)] = (mine + left_in[t - 1, :, sub(q)].astype(F32)).astype(BF16)

                @pl.when(z == last)
                def _():
                    left_out[t, :, sub(q)] = mine.astype(BF16)
            left_copy(t, q).start()

    cntr_copy = pltpu.make_async_remote_copy(
        cnt_to_right, cnt_right, cntr_sem.at[0], cntr_sem.at[1], device_id=(dp + 2, cd), device_id_type=MESH)
    cntl_copy = pltpu.make_async_remote_copy(
        cnt_to_left, cnt_left, cntl_sem.at[0], cntl_sem.at[1], device_id=(dp - 2, cd), device_id_type=MESH)

    for t in range(last):
        for q in range(SUBS):
            if t == 0:
                pair_copy(q).wait_recv()
                own[:, sub(q)] += pair_in[:, sub(q)].astype(F32)
            right_step(t, q)
            left_step(t, q)
        if t == 0:
            cntp_copy.wait_recv()
            cnt_pair[...] += cnt[...]

            zq_copy.wait_recv()
            share_q = (plane_q * mine_factor + zq_in[...].astype(F32) * other_factor) * inverse
            q_all[xy] = share_q.astype(BF16)

            def qa_copy(i):
                j, device = peer(i)
                return pltpu.make_async_remote_copy(
                    q_all.at[xy], q_all.at[xy], qa_s.at[i], qa_r.at[xy], device_id=device, device_id_type=MESH)

            def qa_wait(i):
                j, device = peer(i)
                pltpu.make_async_remote_copy(
                    q_all.at[j], q_all.at[j], qa_s.at[i], qa_r.at[j], device_id=device, device_id_type=MESH).wait_recv()

            each(lambda i: qa_copy(i).start())

        @pl.when(t == z)
        def _():
            if t == 0:
                cnt_to_right[...] = cnt_pair[...]
            else:
                cntr_copy.wait_recv()
                cnt_to_right[...] = cnt_pair[...] + cnt_right[...]
            cntr_copy.start()

        @pl.when(t == last - z)
        def _():
            if t == 0:
                cnt_to_left[...] = cnt_pair[...]
            else:
                cntl_copy.wait_recv()
                cnt_to_left[...] = cnt_pair[...] + cnt_left[...]
            cntl_copy.start()

    each(qa_wait)
    quant_ref[...] = q_all[...].reshape(WIDTH, ROWS).T

    @pl.when(z == 0)
    def _():
        cntl_copy.wait_recv()
        counts_ref[...] = cnt_pair[...] + cnt_left[...]

    @pl.when(z == last)
    def _():
        cntr_copy.wait_recv()
        counts_ref[...] = cnt_pair[...] + cnt_right[...]

    @pl.when((z > 0) & (z < last))
    def _():
        counts_ref[...] = cnt_pair[...] + cnt_left[...] + cnt_right[...]

    counts_ref[...] = 0.9 * old_counts_ref[...] + 0.1 * counts_ref[...]

    for q in range(SUBS):
        @pl.when(z > 0)
        def _():
            right_copy(last - 1, q).wait_recv()
            own[share(z), sub(q)] += right_in[last - 1, :, sub(q)].astype(F32)

        @pl.when(z < last)
        def _():
            left_copy(last - 1, q).wait_recv()
            own[share(z), sub(q)] += left_in[last - 1, :, sub(q)].astype(F32)

        sums_next = 0.9 * old_sums_ref[:, sub(q)] + 0.1 * own[share(z), sub(q)]
        next_ref[:, sub(q)] = sums_next / counts_ref[:, sub(q)]

    each(lambda i: stat_copy(i).wait_send())
    each(lambda i: q_copy(i).wait_send())
    each(lambda i: qa_copy(i).wait_send())
    zstat_copy.wait_send()
    zq_copy.wait_send()
    cntp_copy.wait_send()
    for q in range(SUBS):
        pair_copy(q).wait_send()

    @pl.when(z < last)
    def _():
        cntr_copy.wait_send()

    @pl.when(z > 0)
    def _():
        cntl_copy.wait_send()

    for t in range(last):
        @pl.when(t >= z)
        def _():
            for q in range(SUBS):
                right_copy(t, q).wait_send()

        @pl.when(t >= last - z)
        def _():
            for q in range(SUBS):
                left_copy(t, q).wait_send()


def body(latents, codebook, old_counts, old_sums):
    any_spec = pl.BlockSpec(memory_space=pl.ANY)
    vmem_spec = pl.BlockSpec(memory_space=pltpu.VMEM)
    dma = pltpu.SemaphoreType.DMA
    quantized, counts_next, codebook_next = pl.pallas_call(
        kernel,
        out_shape=(
            jax.ShapeDtypeStruct((ROWS, WIDTH), BF16),
            jax.ShapeDtypeStruct((1, CODES), F32),
            jax.ShapeDtypeStruct((SHARE, CODES), F32),
        ),
        in_specs=[any_spec, any_spec, vmem_spec, vmem_spec],
        out_specs=(vmem_spec, vmem_spec, vmem_spec),
        scratch_shapes=[
            pltpu.VMEM((ROWS, WIDTH), BF16),
            pltpu.VMEM((WIDTH, ROWS), BF16),
            pltpu.VMEM((CODES, WIDTH), BF16),
            pltpu.VMEM((WIDTH, CODES), BF16),
            pltpu.VMEM((CODES, ROWS), F32),
            pltpu.VMEM((CODES, ROWS), BF16),
            pltpu.VMEM((PLANE, 2, ROWS), F32),
            pltpu.VMEM((2, ROWS), F32),
            pltpu.VMEM((2, ROWS), F32),
            pltpu.VMEM((WIDTH, ROWS), F32),
            pltpu.VMEM((WIDTH, ROWS), BF16),
            pltpu.VMEM((PLANE, PIECE, ROWS), BF16),
            pltpu.VMEM((PIECE, ROWS), BF16),
            pltpu.VMEM((PIECE, ROWS), BF16),
            pltpu.VMEM((PLANE, PIECE, ROWS), BF16),
            pltpu.VMEM((WIDTH + SHARE, ROWS), BF16),
            pltpu.VMEM((HALF, CODES), F32),
            pltpu.VMEM((HALF, CODES), BF16),
            pltpu.VMEM((HALF, CODES), BF16),
            pltpu.VMEM((1, CODES), F32),
            pltpu.VMEM((1, CODES), F32),
            pltpu.VMEM((1, CODES), F32),
            pltpu.VMEM((1, CODES), F32),
            pltpu.VMEM((1, CODES), F32),
            pltpu.VMEM((1, CODES), F32),
            pltpu.VMEM((LINE - 1, SHARE, CODES), BF16),
            pltpu.VMEM((LINE - 1, SHARE, CODES), BF16),
            pltpu.VMEM((LINE - 1, SHARE, CODES), BF16),
            pltpu.VMEM((LINE - 1, SHARE, CODES), BF16),
            dma,
            dma((BLOCKS,)),
            dma((PLANE,)),
            dma((PLANE,)),
            dma((2,)),
            dma((PLANE,)),
            dma((PLANE,)),
            dma((2,)),
            dma((PLANE,)),
            dma((PLANE,)),
            dma((SUBS,)),
            dma((SUBS,)),
            dma((2,)),
            dma((2,)),
            dma((2,)),
            dma((LINE - 1, SUBS)),
            dma((LINE - 1, SUBS)),
            dma((LINE - 1, SUBS)),
            dma((LINE - 1, SUBS)),
        ],
        compiler_params=pltpu.CompilerParams(
            collective_id=0, has_side_effects=True, vmem_limit_bytes=60 * 1024 * 1024),
        cost_estimate=pl.CostEstimate(flops=6_500_000_000, bytes_accessed=4_000_000, transcendentals=4_200_000),
    )(latents, codebook, old_counts.reshape(1, CODES), old_sums)
    return quantized, counts_next.reshape(CODES), codebook_next


def solution(mesh):
    return jax.shard_map(
        body,
        mesh=mesh,
        in_specs=(P("dp", None), P("code", None), P("code"), P("dp", "code")),
        out_specs=(P("dp", None), P("code"), P("dp", "code")),
        check_vma=False,
    )
```

```python
import math

import jax
import jax.numpy as jnp
from jax import lax
from jax.experimental import pallas as pl
from jax.experimental.pallas import tpu as pltpu
from jax.sharding import PartitionSpec as P

MESH = pl.DeviceIdType.MESH
F32 = jnp.float32
BF16 = jnp.bfloat16

ROWS = 1024
CODES = 4096
WIDTH = 256
BLOCK = 512
BLOCKS = CODES // BLOCK
PLANE = 16
PIECE = WIDTH // PLANE
LINE = 8
SUBS = 4
SUB = CODES // SUBS
SHARE = 16
HALF = SHARE * LINE


def dot(a, b):
    return lax.dot_general(a, b, (((1,), (0,)), ((), ())), preferred_element_type=F32)


def dot_t(a, b):
    return lax.dot_general(a, b, (((1,), (1,)), ((), ())), preferred_element_type=F32)


def kernel(
    latents_hbm, codebook_hbm, quant_ref, counts_ref, sums_ref,
    lat, lat_t, code, code_t, logits, raised,
    stat_in, zstat_out, zstat_in,
    q_part, q_send, q_in, zq_out, zq_in, q_all,
    scaled, own, pair_out, pair_in, cnt, cnt_pair, cnt_right, cnt_left, cnt_to_right, cnt_to_left,
    right_in, left_in, right_out, left_out,
    lat_sem, code_sem,
    stat_s, stat_r, zstat_sem, q_s, q_r, zq_sem, qa_s, qa_r,
    pair_s, pair_r, cntp_sem, cntr_sem, cntl_sem, right_s, right_r, left_s, left_r,
):
    dp = lax.axis_index("dp")
    cd = lax.axis_index("code")
    z = dp // 2
    core = dp % 2
    zh = cd // PLANE
    xy = cd % PLANE
    partner = (dp + 1 - 2 * core, cd)
    across = (dp, (1 - zh) * PLANE + xy)

    def peer(i):
        j = (xy + i) % PLANE
        return j, (dp, zh * PLANE + j)

    lat_copy = pltpu.make_async_copy(latents_hbm, lat, lat_sem)
    lat_copy.start()

    def code_copy(b):
        rows = pl.ds(pl.multiple_of(b * BLOCK, BLOCK), BLOCK)
        return pltpu.make_async_copy(codebook_hbm.at[rows], code.at[rows], code_sem.at[b])

    for b in range(BLOCKS):
        code_copy(b).start()

    barrier = pltpu.get_barrier_semaphore()

    def greet(i, carry):
        pl.semaphore_signal(barrier, inc=1, device_id=peer(i)[1], device_id_type=MESH)
        return carry

    lax.fori_loop(1, PLANE, greet, 0)
    pl.semaphore_signal(barrier, inc=1, device_id=partner, device_id_type=MESH)
    pl.semaphore_signal(barrier, inc=1, device_id=across, device_id_type=MESH)

    @pl.when(z > 0)
    def _():
        pl.semaphore_signal(barrier, inc=1, device_id=(dp - 2, cd), device_id_type=MESH)

    @pl.when(z < LINE - 1)
    def _():
        pl.semaphore_signal(barrier, inc=1, device_id=(dp + 2, cd), device_id_type=MESH)

    lat_copy.wait()
    lat_t[...] = lat[...].T

    per_dot = 2.0 * 2.0 / math.sqrt(WIDTH) * math.log2(math.e)
    per_norm = 2.0 / math.sqrt(WIDTH) * math.log2(math.e)

    def first(b, top):
        code_copy(b).wait()
        rows = pl.ds(pl.multiple_of(b * BLOCK, BLOCK), BLOCK)
        block = code[rows, :]
        wide = block.astype(F32)
        norms = jnp.sum(wide * wide, axis=1, keepdims=True) * per_norm
        part = dot(block, lat_t[...]) * per_dot - norms
        logits[rows, :] = part
        code_t[:, rows] = block.T
        return jnp.maximum(top, jnp.max(part.reshape(BLOCK // 8, 8, ROWS), axis=0))

    top = lax.fori_loop(0, BLOCKS, first, jnp.full((8, ROWS), -jnp.inf, F32))
    top = jnp.max(top, axis=0, keepdims=True)

    def second(b, total):
        rows = pl.ds(pl.multiple_of(b * BLOCK, BLOCK), BLOCK)
        part = jnp.exp2(logits[rows, :] - top)
        low = part.astype(BF16)
        raised[rows, :] = low
        return total + jnp.sum(part.reshape(BLOCK // 8, 8, ROWS), axis=0)

    total = lax.fori_loop(0, BLOCKS, second, jnp.zeros((8, ROWS), F32))
    total = jnp.sum(total, axis=0, keepdims=True)

    stat_in[xy] = top + jnp.log2(total)
    ends = (z == 0) | (z == LINE - 1)

    @pl.when(ends)
    def _():
        pl.semaphore_wait(barrier, PLANE + 2)

    @pl.when(jnp.logical_not(ends))
    def _():
        pl.semaphore_wait(barrier, PLANE + 3)

    def stat_copy(i):
        j, device = peer(i)
        return pltpu.make_async_remote_copy(
            stat_in.at[xy], stat_in.at[xy], stat_s.at[i], stat_r.at[xy], device_id=device, device_id_type=MESH)

    def stat_wait(i):
        j, device = peer(i)
        pltpu.make_async_remote_copy(
            stat_in.at[j], stat_in.at[j], stat_s.at[i], stat_r.at[j], device_id=device, device_id_type=MESH).wait_recv()

    def each(run):
        def step(i, carry):
            run(i)
            return carry
        lax.fori_loop(1, PLANE, step, 0)

    each(lambda i: stat_copy(i).start())

    q_send[...] = (dot(code_t[...], raised[...]) * (1.0 / total)).astype(BF16)

    def piece(j):
        return pl.ds(pl.multiple_of(j * PIECE, PIECE), PIECE)

    def q_copy(i):
        j, device = peer(i)
        return pltpu.make_async_remote_copy(
            q_send.at[piece(j)], q_in.at[xy], q_s.at[i], q_r.at[xy], device_id=device, device_id_type=MESH)

    def q_wait(i):
        j, device = peer(i)
        pltpu.make_async_remote_copy(
            q_send.at[piece(j)], q_in.at[j], q_s.at[i], q_r.at[j], device_id=device, device_id_type=MESH).wait_recv()

    each(lambda i: q_copy(i).start())
    q_in[xy] = q_send[piece(xy), :]

    each(stat_wait)
    plane_top = stat_in[0]
    for j in range(1, PLANE):
        plane_top = jnp.maximum(plane_top, stat_in[j])
    plane_total = jnp.zeros((1, ROWS), F32)
    for j in range(PLANE):
        plane_total += jnp.exp2(stat_in[j] - plane_top)
    plane_log = plane_top + jnp.log2(plane_total)
    zstat_out[...] = plane_log
    zstat_copy = pltpu.make_async_remote_copy(
        zstat_out, zstat_in, zstat_sem.at[0], zstat_sem.at[1], device_id=across, device_id_type=MESH)
    zstat_copy.start()

    zstat_copy.wait_recv()
    other_log = zstat_in[...]
    full_top = jnp.maximum(plane_log, other_log)
    full_log = full_top + jnp.log2(jnp.exp2(plane_log - full_top) + jnp.exp2(other_log - full_top))
    factor = jnp.exp2(top - full_log)

    for side in range(2):
        which = core if side == 0 else 1 - core
        for c in range(LINE):
            src = pl.ds(pl.multiple_of(c * 2 * SHARE + which * SHARE, SHARE), SHARE)
            scaled[side * HALF + c * SHARE : side * HALF + (c + 1) * SHARE, :] = (
                lat_t[src, :].astype(F32) * factor).astype(BF16)
    high = factor.astype(BF16)
    rest = (factor - high.astype(F32)).astype(BF16)
    line_no = lax.broadcasted_iota(jnp.int32, (SHARE, ROWS), 0)
    scaled[WIDTH : WIDTH + SHARE, :] = jnp.where(
        line_no == 0, high.astype(F32), jnp.where(line_no == 1, rest.astype(F32), 0.0)).astype(BF16)

    def sub(q):
        return pl.ds(q * SUB, SUB)

    def pair_copy(q):
        return pltpu.make_async_remote_copy(
            pair_out.at[:, sub(q)], pair_in.at[:, sub(q)], pair_s.at[q], pair_r.at[q],
            device_id=partner, device_id_type=MESH)

    for q in range(SUBS):
        sums = dot_t(scaled[...], raised[sub(q), :])
        pair_out[:, sub(q)] = sums[HALF:WIDTH].astype(BF16)
        pair_copy(q).start()
        own[:, sub(q)] = sums[0:HALF]
        cnt[:, sub(q)] = sums[WIDTH : WIDTH + 1] + sums[WIDTH + 1 : WIDTH + 2]

    cntp_copy = pltpu.make_async_remote_copy(
        cnt, cnt_pair, cntp_sem.at[0], cntp_sem.at[1], device_id=partner, device_id_type=MESH)
    cntp_copy.start()

    def right_copy(t, q):
        return pltpu.make_async_remote_copy(
            right_out.at[t, :, sub(q)], right_in.at[t, :, sub(q)], right_s.at[t, q], right_r.at[t, q],
            device_id=(dp + 2, cd), device_id_type=MESH)

    def left_copy(t, q):
        return pltpu.make_async_remote_copy(
            left_out.at[t, :, sub(q)], left_in.at[t, :, sub(q)], left_s.at[t, q], left_r.at[t, q],
            device_id=(dp - 2, cd), device_id_type=MESH)

    def share(c):
        return pl.ds(pl.multiple_of(c * SHARE, SHARE), SHARE)

    last = LINE - 1

    def right_step(t, q):
        @pl.when(t >= z)
        def _():
            mine = own[share(last - t + z), sub(q)]
            if t == 0:
                right_out[t, :, sub(q)] = mine.astype(BF16)
            else:
                @pl.when(z > 0)
                def _():
                    right_copy(t - 1, q).wait_recv()
                    right_out[t, :, sub(q)] = (mine + right_in[t - 1, :, sub(q)].astype(F32)).astype(BF16)

                @pl.when(z == 0)
                def _():
                    right_out[t, :, sub(q)] = mine.astype(BF16)
            right_copy(t, q).start()

    def left_step(t, q):
        @pl.when(t >= last - z)
        def _():
            mine = own[share(t - last + z), sub(q)]
            if t == 0:
                left_out[t, :, sub(q)] = mine.astype(BF16)
            else:
                @pl.when(z < last)
                def _():
                    left_copy(t - 1, q).wait_recv()
                    left_out[t, :, sub(q)] = (mine + left_in[t - 1, :, sub(q)].astype(F32)).astype(BF16)

                @pl.when(z == last)
                def _():
                    left_out[t, :, sub(q)] = mine.astype(BF16)
            left_copy(t, q).start()

    cntr_copy = pltpu.make_async_remote_copy(
        cnt_to_right, cnt_right, cntr_sem.at[0], cntr_sem.at[1], device_id=(dp + 2, cd), device_id_type=MESH)
    cntl_copy = pltpu.make_async_remote_copy(
        cnt_to_left, cnt_left, cntl_sem.at[0], cntl_sem.at[1], device_id=(dp - 2, cd), device_id_type=MESH)

    for t in range(last):
        for q in range(SUBS):
            if t == 0:
                pair_copy(q).wait_recv()
                own[:, sub(q)] += pair_in[:, sub(q)].astype(F32)
            right_step(t, q)
            left_step(t, q)
        if t == 0:
            cntp_copy.wait_recv()
            cnt_pair[...] += cnt[...]

            each(q_wait)
            plane_q = jnp.zeros((PIECE, ROWS), F32)
            for j in range(PLANE):
                plane_q += q_in[j].astype(F32) * jnp.exp2(stat_in[j] - full_log)
            q_part[...] = plane_q
            zq_out[...] = plane_q.astype(BF16)
            zq_copy = pltpu.make_async_remote_copy(
                zq_out, zq_in, zq_sem.at[0], zq_sem.at[1], device_id=across, device_id_type=MESH)
            zq_copy.start()

        if t == 3:
            zq_copy.wait_recv()
            q_all[xy] = (q_part[...] + zq_in[...].astype(F32)).astype(BF16)

            def qa_copy(i):
                j, device = peer(i)
                return pltpu.make_async_remote_copy(
                    q_all.at[xy], q_all.at[xy], qa_s.at[i], qa_r.at[xy], device_id=device, device_id_type=MESH)

            def qa_wait(i):
                j, device = peer(i)
                pltpu.make_async_remote_copy(
                    q_all.at[j], q_all.at[j], qa_s.at[i], qa_r.at[j], device_id=device, device_id_type=MESH).wait_recv()

            each(lambda i: qa_copy(i).start())

        @pl.when(t == z)
        def _():
            if t == 0:
                cnt_to_right[...] = cnt_pair[...]
            else:
                cntr_copy.wait_recv()
                cnt_to_right[...] = cnt_pair[...] + cnt_right[...]
            cntr_copy.start()

        @pl.when(t == last - z)
        def _():
            if t == 0:
                cnt_to_left[...] = cnt_pair[...]
            else:
                cntl_copy.wait_recv()
                cnt_to_left[...] = cnt_pair[...] + cnt_left[...]
            cntl_copy.start()

    each(qa_wait)
    quant_ref[...] = q_all[...]

    @pl.when(z == 0)
    def _():
        cntl_copy.wait_recv()
        counts_ref[...] = cnt_pair[...] + cnt_left[...]

    @pl.when(z == last)
    def _():
        cntr_copy.wait_recv()
        counts_ref[...] = cnt_pair[...] + cnt_right[...]

    @pl.when((z > 0) & (z < last))
    def _():
        counts_ref[...] = cnt_pair[...] + cnt_left[...] + cnt_right[...]

    for q in range(SUBS):
        @pl.when(z > 0)
        def _():
            right_copy(last - 1, q).wait_recv()
            own[share(z), sub(q)] += right_in[last - 1, :, sub(q)].astype(F32)

        @pl.when(z < last)
        def _():
            left_copy(last - 1, q).wait_recv()
            own[share(z), sub(q)] += left_in[last - 1, :, sub(q)].astype(F32)

        sums_ref[:, sub(q)] = own[share(z), sub(q)]

    each(lambda i: stat_copy(i).wait_send())
    each(lambda i: q_copy(i).wait_send())
    each(lambda i: qa_copy(i).wait_send())
    zstat_copy.wait_send()
    zq_copy.wait_send()
    cntp_copy.wait_send()
    for q in range(SUBS):
        pair_copy(q).wait_send()

    @pl.when(z < last)
    def _():
        cntr_copy.wait_send()

    @pl.when(z > 0)
    def _():
        cntl_copy.wait_send()

    for t in range(last):
        @pl.when(t >= z)
        def _():
            for q in range(SUBS):
                right_copy(t, q).wait_send()

        @pl.when(t >= last - z)
        def _():
            for q in range(SUBS):
                left_copy(t, q).wait_send()


def finish(quant_t_ref, counts_ref, sums_ref, old_counts_ref, old_sums_ref, quant_ref, counts_next_ref, next_ref):
    quant_ref[...] = quant_t_ref[...].reshape(WIDTH, ROWS).T
    counts_next = 0.9 * old_counts_ref[...] + 0.1 * counts_ref[...]
    counts_next_ref[...] = counts_next
    next_ref[...] = (0.9 * old_sums_ref[...] + 0.1 * sums_ref[...]) / counts_next


def body(latents, codebook, old_counts, old_sums):
    any_spec = pl.BlockSpec(memory_space=pl.ANY)
    vmem_spec = pl.BlockSpec(memory_space=pltpu.VMEM)
    dma = pltpu.SemaphoreType.DMA
    quant_t, counts, code_sums = pl.pallas_call(
        kernel,
        out_shape=(
            jax.ShapeDtypeStruct((PLANE, PIECE, ROWS), BF16),
            jax.ShapeDtypeStruct((1, CODES), F32),
            jax.ShapeDtypeStruct((SHARE, CODES), F32),
        ),
        in_specs=[any_spec, any_spec],
        out_specs=(vmem_spec, vmem_spec, vmem_spec),
        scratch_shapes=[
            pltpu.VMEM((ROWS, WIDTH), BF16),
            pltpu.VMEM((WIDTH, ROWS), BF16),
            pltpu.VMEM((CODES, WIDTH), BF16),
            pltpu.VMEM((WIDTH, CODES), BF16),
            pltpu.VMEM((CODES, ROWS), F32),
            pltpu.VMEM((CODES, ROWS), BF16),
            pltpu.VMEM((PLANE, 1, ROWS), F32),
            pltpu.VMEM((1, ROWS), F32),
            pltpu.VMEM((1, ROWS), F32),
            pltpu.VMEM((PIECE, ROWS), F32),
            pltpu.VMEM((WIDTH, ROWS), BF16),
            pltpu.VMEM((PLANE, PIECE, ROWS), BF16),
            pltpu.VMEM((PIECE, ROWS), BF16),
            pltpu.VMEM((PIECE, ROWS), BF16),
            pltpu.VMEM((PLANE, PIECE, ROWS), BF16),
            pltpu.VMEM((WIDTH + SHARE, ROWS), BF16),
            pltpu.VMEM((HALF, CODES), F32),
            pltpu.VMEM((HALF, CODES), BF16),
            pltpu.VMEM((HALF, CODES), BF16),
            pltpu.VMEM((1, CODES), F32),
            pltpu.VMEM((1, CODES), F32),
            pltpu.VMEM((1, CODES), F32),
            pltpu.VMEM((1, CODES), F32),
            pltpu.VMEM((1, CODES), F32),
            pltpu.VMEM((1, CODES), F32),
            pltpu.VMEM((LINE - 1, SHARE, CODES), BF16),
            pltpu.VMEM((LINE - 1, SHARE, CODES), BF16),
            pltpu.VMEM((LINE - 1, SHARE, CODES), BF16),
            pltpu.VMEM((LINE - 1, SHARE, CODES), BF16),
            dma,
            dma((BLOCKS,)),
            dma((PLANE,)),
            dma((PLANE,)),
            dma((2,)),
            dma((PLANE,)),
            dma((PLANE,)),
            dma((2,)),
            dma((PLANE,)),
            dma((PLANE,)),
            dma((SUBS,)),
            dma((SUBS,)),
            dma((2,)),
            dma((2,)),
            dma((2,)),
            dma((LINE - 1, SUBS)),
            dma((LINE - 1, SUBS)),
            dma((LINE - 1, SUBS)),
            dma((LINE - 1, SUBS)),
        ],
        compiler_params=pltpu.CompilerParams(
            collective_id=0, has_side_effects=True, vmem_limit_bytes=60 * 1024 * 1024),
        cost_estimate=pl.CostEstimate(flops=6_500_000_000, bytes_accessed=4_000_000, transcendentals=4_200_000),
    )(latents, codebook)
    quantized, counts_next, codebook_next = pl.pallas_call(
        finish,
        out_shape=(
            jax.ShapeDtypeStruct((ROWS, WIDTH), BF16),
            jax.ShapeDtypeStruct((1, CODES), F32),
            jax.ShapeDtypeStruct((SHARE, CODES), F32),
        ),
        in_specs=[vmem_spec] * 5,
        out_specs=(vmem_spec, vmem_spec, vmem_spec),
        cost_estimate=pl.CostEstimate(flops=300_000, bytes_accessed=2_000_000, transcendentals=0),
    )(quant_t, counts, code_sums, old_counts.reshape(1, CODES), old_sums)
    return quantized, counts_next.reshape(CODES), codebook_next


def solution(mesh):
    return jax.shard_map(
        body,
        mesh=mesh,
        in_specs=(P("dp", None), P("code", None), P("code"), P("dp", "code")),
        out_specs=(P("dp", None), P("code"), P("dp", "code")),
        check_vma=False,
    )
```

```python
import math

import jax
import jax.numpy as jnp
from jax import lax
from jax.experimental import pallas as pl
from jax.experimental.pallas import tpu as pltpu
from jax.sharding import PartitionSpec as P

MESH = pl.DeviceIdType.MESH
F32 = jnp.float32
BF16 = jnp.bfloat16

ROWS = 1024
CODES = 4096
WIDTH = 256
BLOCK = 2048
BLOCKS = CODES // BLOCK
PLANE = 16
STRIP = ROWS // PLANE
PIECE = WIDTH // PLANE
LINE = 8
PART = CODES // 2
SUBS = 2
SUB = PART // SUBS
SHARE = 16
HALF = SHARE * LINE
QSTEP = 3
CSTEP = 3


def dot(a, b):
    return lax.dot_general(a, b, (((1,), (0,)), ((), ())), preferred_element_type=F32)


def dot_t(a, b):
    return lax.dot_general(a, b, (((1,), (1,)), ((), ())), preferred_element_type=F32)


def kernel(
    latents_hbm, codebook_hbm, quant_ref, counts_ref, sums_ref,
    lat, lat_t, lat2, lat2_t, code, code_t, logits, raised, raised2,
    stat_in, zstat_out, zstat_in,
    q_send, q_in, zq_out, zq_in, q_all,
    scaled, scaled2, own, pair_out, pair_in, cnt, cnt_pair, cnt_line, cnt_half,
    in_in, in_out, out_in, out_out, direct_in,
    lat_sem, code_sem, strip_s, strip_r, spread_s, spread_r,
    stat_s, stat_r, zstat_s, zstat_r, q_s, q_r, zq_sem, qa_s, qa_r,
    pair_s, pair_r, cntp_sem, cnt_s, cnt_r, half_sem, in_s, in_r, out_s, out_r, direct_r, ready,
):
    dp = lax.axis_index("dp")
    cd = lax.axis_index("code")
    z = dp // 2
    core = dp % 2
    zh = cd // PLANE
    xy = cd % PLANE
    partner = (dp + 1 - 2 * core, cd)
    cd_across = (1 - zh) * PLANE + xy
    across = (dp, cd_across)
    dp_pair = (dp + LINE) % (2 * LINE)
    part = z // 4
    place = z + part * (7 - 2 * z)
    relatives = (across, (dp_pair, cd), (dp_pair, cd_across))

    middle = ((4 - part) * 2 + core, cd)

    def mate(i):
        return ((part * 4 + (z + i) % 4) * 2 + core, cd)

    def peer(i):
        j = (xy + i) % PLANE
        return j, (dp, zh * PLANE + j)

    lat_copy = pltpu.make_async_copy(latents_hbm, lat, lat_sem)
    lat_copy.start()

    def code_copy(b):
        rows = pl.ds(pl.multiple_of(b * BLOCK, BLOCK), BLOCK)
        return pltpu.make_async_copy(codebook_hbm.at[rows], code.at[rows], code_sem.at[b])

    for b in range(BLOCKS):
        code_copy(b).start()

    barrier = pltpu.get_barrier_semaphore()

    def greet(i, carry):
        pl.semaphore_signal(barrier, inc=1, device_id=peer(i)[1], device_id_type=MESH)
        return carry

    lax.fori_loop(1, PLANE, greet, 0)
    greeted = [partner, (dp_pair, cd)] + [mate(i) for i in (1, 2, 3)]
    for device in greeted:
        pl.semaphore_signal(barrier, inc=1, device_id=device, device_id_type=MESH)

    @pl.when(place > 0)
    def _():
        pl.semaphore_signal(barrier, inc=1, device_id=middle, device_id_type=MESH)

    @pl.when(zh == 0)
    def _():
        for device in (across, (dp_pair, cd_across)):
            pl.semaphore_signal(barrier, inc=1, device_id=device, device_id_type=MESH)

    lat_copy.wait()
    lat_t[...] = lat[...].T
    per_dot = 2.0 * 2.0 / math.sqrt(WIDTH) * math.log2(math.e)
    per_norm = 2.0 / math.sqrt(WIDTH) * math.log2(math.e)

    def first(b, top):
        code_copy(b).wait()
        rows = pl.ds(pl.multiple_of(b * BLOCK, BLOCK), BLOCK)
        block = code[rows, :]
        wide = block.astype(F32)
        norms = jnp.sum(wide * wide, axis=1, keepdims=True) * per_norm
        part = dot(block, lat_t[...]) * per_dot - norms
        logits[rows, :] = part
        code_t[:, rows] = block.T
        return jnp.maximum(top, jnp.max(part.reshape(BLOCK // 8, 8, ROWS), axis=0))

    top = lax.fori_loop(0, BLOCKS, first, jnp.full((8, ROWS), -jnp.inf, F32))
    top = jnp.max(top, axis=0, keepdims=True)

    near = PLANE - 1 + 2 + 3
    for side in range(2):
        for mid in range(2):
            @pl.when((zh == side) & ((place == 3) == (mid == 1)))
            def _():
                pl.semaphore_wait(barrier, near + 2 * side + 3 * mid)

    @pl.when(zh == 1)
    def _():
        for device in (across, (dp_pair, cd_across)):
            pl.semaphore_signal(ready, inc=1, device_id=device, device_id_type=MESH)

    def strip(j):
        return pl.ds(pl.multiple_of(j * STRIP, STRIP), STRIP)

    strip_copy = pltpu.make_async_remote_copy(
        lat.at[strip(xy)], lat2.at[strip(xy)], strip_s, strip_r, device_id=(dp_pair, cd), device_id_type=MESH)
    strip_copy.start()

    def second(b, total):
        rows = pl.ds(pl.multiple_of(b * BLOCK, BLOCK), BLOCK)
        part = jnp.exp2(logits[rows, :] - top)
        low = part.astype(BF16)
        raised[rows, :] = low
        return total + jnp.sum(part.reshape(BLOCK // 8, 8, ROWS), axis=0)

    total = lax.fori_loop(0, BLOCKS, second, jnp.zeros((8, ROWS), F32))
    total = jnp.sum(total, axis=0, keepdims=True)

    stat_in[xy] = top + jnp.log2(total)
    def stat_copy(i):
        j, device = peer(i)
        return pltpu.make_async_remote_copy(
            stat_in.at[xy], stat_in.at[xy], stat_s.at[i], stat_r.at[xy], device_id=device, device_id_type=MESH)

    def stat_wait(i):
        j, device = peer(i)
        pltpu.make_async_remote_copy(
            stat_in.at[j], stat_in.at[j], stat_s.at[i], stat_r.at[j], device_id=device, device_id_type=MESH).wait_recv()

    def each(run):
        def step(i, carry):
            run(i)
            return carry
        lax.fori_loop(1, PLANE, step, 0)

    each(lambda i: stat_copy(i).start())

    q_send[...] = (dot(code_t[...], raised[...]) * (1.0 / total)).astype(BF16)

    def piece(j):
        return pl.ds(pl.multiple_of(j * PIECE, PIECE), PIECE)

    def q_copy(i):
        j, device = peer(i)
        return pltpu.make_async_remote_copy(
            q_send.at[piece(j)], q_in.at[xy], q_s.at[i], q_r.at[xy], device_id=device, device_id_type=MESH)

    def q_wait(i):
        j, device = peer(i)
        pltpu.make_async_remote_copy(
            q_send.at[piece(j)], q_in.at[j], q_s.at[i], q_r.at[j], device_id=device, device_id_type=MESH).wait_recv()

    def spread_copy(i):
        j, device = peer(i)
        return pltpu.make_async_remote_copy(
            lat2.at[strip(xy)], lat2.at[strip(xy)], spread_s.at[i], spread_r.at[xy], device_id=device, device_id_type=MESH)

    def spread_wait(i):
        j, device = peer(i)
        pltpu.make_async_remote_copy(
            lat2.at[strip(j)], lat2.at[strip(j)], spread_s.at[i], spread_r.at[j], device_id=device, device_id_type=MESH).wait_recv()

    each(lambda i: q_copy(i).start())
    strip_copy.wait_recv()
    each(lambda i: spread_copy(i).start())

    q_in[xy] = q_send[piece(xy), :]

    each(stat_wait)
    plane_top = stat_in[0]
    for j in range(1, PLANE):
        plane_top = jnp.maximum(plane_top, stat_in[j])
    plane_total = jnp.zeros((1, ROWS), F32)
    for j in range(PLANE):
        plane_total += jnp.exp2(stat_in[j] - plane_top)
    plane_log = plane_top + jnp.log2(plane_total)
    zstat_out[...] = plane_log

    def zstat_copy(k):
        return pltpu.make_async_remote_copy(
            zstat_out, zstat_in.at[k], zstat_s.at[k], zstat_r.at[k], device_id=relatives[k], device_id_type=MESH)

    @pl.when(zh == 0)
    def _():
        pl.semaphore_wait(ready, 2)

    for k in range(3):
        zstat_copy(k).start()

    each(q_wait)
    plane_q = jnp.zeros((PIECE, ROWS), F32)
    for j in range(PLANE):
        plane_q += q_in[j].astype(F32) * jnp.exp2(stat_in[j] - plane_log)
    zq_out[...] = plane_q.astype(BF16)
    zq_copy = pltpu.make_async_remote_copy(
        zq_out, zq_in, zq_sem.at[0], zq_sem.at[1], device_id=across, device_id_type=MESH)
    zq_copy.start()

    each(spread_wait)
    lat2_t[...] = lat2[...].T
    start = pl.multiple_of(part * PART, PART)
    block = code[pl.ds(start, PART), :]
    wide = block.astype(F32)
    norms = jnp.sum(wide * wide, axis=1, keepdims=True) * per_norm
    logits2 = dot(block, lat2_t[...]) * per_dot - norms
    logits[0:PART, :] = logits2
    top2 = jnp.max(jnp.max(logits2.reshape(PART // 8, 8, ROWS), axis=0), axis=0, keepdims=True)
    raised2[...] = jnp.exp2(logits[0:PART, :] - top2).astype(BF16)

    def log_sum(a, b):
        high = jnp.maximum(a, b)
        return high + jnp.log2(jnp.exp2(a - high) + jnp.exp2(b - high))

    for k in range(3):
        zstat_copy(k).wait_recv()
    full_log = log_sum(plane_log, zstat_in[0])
    factor = jnp.exp2(top - full_log)
    factor2 = jnp.exp2(top2 - log_sum(zstat_in[1], zstat_in[2]))

    line_no = lax.broadcasted_iota(jnp.int32, (SHARE, ROWS), 0)
    for out, rows_t, by in ((scaled, lat_t, factor), (scaled2, lat2_t, factor2)):
        for side in range(2):
            which = core if side == 0 else 1 - core
            for e in range(LINE):
                chip = e + part * (LINE - 1 - 2 * e)
                src = pl.ds(pl.multiple_of(chip * 2 * SHARE + which * SHARE, SHARE), SHARE)
                out[side * HALF + e * SHARE : side * HALF + (e + 1) * SHARE, :] = (
                    rows_t[src, :].astype(F32) * by).astype(BF16)
        high = by.astype(BF16).astype(F32)
        out[WIDTH : WIDTH + SHARE, :] = jnp.where(
            line_no == 0, high, jnp.where(line_no == 1, by - high, 0.0)).astype(BF16)

    def sub(q):
        return pl.ds(q * SUB, SUB)

    def pair_copy(q):
        return pltpu.make_async_remote_copy(
            pair_out.at[:, sub(q)], pair_in.at[:, sub(q)], pair_s.at[q], pair_r.at[q],
            device_id=partner, device_id_type=MESH)

    for q in range(SUBS):
        mine = pl.ds(pl.multiple_of(part * PART + q * SUB, SUB), SUB)
        sums = dot_t(scaled[...], raised[mine, :]) + dot_t(scaled2[...], raised2[sub(q), :])
        pair_out[:, sub(q)] = sums[HALF:WIDTH].astype(BF16)
        pair_copy(q).start()
        own[:, sub(q)] = sums[0:HALF]
        cnt[:, sub(q)] = sums[WIDTH : WIDTH + 1] + sums[WIDTH + 1 : WIDTH + 2]

    cntp_copy = pltpu.make_async_remote_copy(
        cnt, cnt_pair, cntp_sem.at[0], cntp_sem.at[1], device_id=partner, device_id_type=MESH)
    cntp_copy.start()

    toward = 2 * (1 - 2 * part)
    last = LINE - 1

    def in_copy(t, q):
        return pltpu.make_async_remote_copy(
            in_out.at[t, :, sub(q)], in_in.at[t, :, sub(q)], in_s.at[t, q], in_r.at[t, q],
            device_id=(dp + toward, cd), device_id_type=MESH)

    def direct_copy(t, q):
        e = 10 - t
        chip = e + part * (last - 2 * e)
        return pltpu.make_async_remote_copy(
            in_out.at[t, :, sub(q)], direct_in.at[:, sub(q)], in_s.at[t, q], direct_r.at[q],
            device_id=(chip * 2 + core, cd), device_id_type=MESH)

    def out_copy(t, q):
        return pltpu.make_async_remote_copy(
            out_out.at[t, :, sub(q)], out_in.at[t, :, sub(q)], out_s.at[t, q], out_r.at[t, q],
            device_id=(dp - toward, cd), device_id_type=MESH)

    def share(e):
        return pl.ds(pl.multiple_of(e * SHARE, SHARE), SHARE)

    def in_step(t, q):
        @pl.when(t >= place)
        def _():
            mine = own[share(last - t + place), sub(q)]

            @pl.when(place == 0)
            def _():
                in_out[t, :, sub(q)] = mine.astype(BF16)

            if t > 0:
                @pl.when(place > 0)
                def _():
                    in_copy(t - 1, q).wait_recv()
                    in_out[t, :, sub(q)] = (mine + in_in[t - 1, :, sub(q)].astype(F32)).astype(BF16)

            @pl.when(place < 3)
            def _():
                in_copy(t, q).start()

            if t >= 3:
                @pl.when(place == 3)
                def _():
                    direct_copy(t, q).start()

    def out_step(t, q):
        @pl.when((place > 0) & (t >= 3 - place))
        def _():
            mine = own[share(t - 3 + place), sub(q)]

            @pl.when(place == 3)
            def _():
                out_out[t, :, sub(q)] = mine.astype(BF16)

            if t > 0:
                @pl.when(place < 3)
                def _():
                    out_copy(t - 1, q).wait_recv()
                    out_out[t, :, sub(q)] = (mine + out_in[t - 1, :, sub(q)].astype(F32)).astype(BF16)

            out_copy(t, q).start()

    def cnt_copy(i):
        return pltpu.make_async_remote_copy(
            cnt_line.at[z % 4], cnt_line.at[z % 4], cnt_s.at[i], cnt_r.at[z % 4], device_id=mate(i), device_id_type=MESH)

    def cnt_wait(i):
        other = (z + i) % 4
        pltpu.make_async_remote_copy(
            cnt_line.at[other], cnt_line.at[other], cnt_s.at[i], cnt_r.at[other],
            device_id=mate(i), device_id_type=MESH).wait_recv()

    half_copy = pltpu.make_async_remote_copy(
        cnt_half.at[0], cnt_half.at[1], half_sem.at[0], half_sem.at[1], device_id=(dp_pair, cd), device_id_type=MESH)

    def qa_copy(i):
        j, device = peer(i)
        return pltpu.make_async_remote_copy(
            q_all.at[xy], q_all.at[xy], qa_s.at[i], qa_r.at[xy], device_id=device, device_id_type=MESH)

    def qa_wait(i):
        j, device = peer(i)
        pltpu.make_async_remote_copy(
            q_all.at[j], q_all.at[j], qa_s.at[i], qa_r.at[j], device_id=device, device_id_type=MESH).wait_recv()

    for t in range(last):
        for q in range(SUBS):
            if t == 0:
                pair_copy(q).wait_recv()
                own[:, sub(q)] += pair_in[:, sub(q)].astype(F32)
            in_step(t, q)
            if t < 3:
                out_step(t, q)
        if t == 0:
            cntp_copy.wait_recv()
            cnt_line[z % 4] = cnt_pair[...] + cnt[...]

            for i in range(1, 4):
                cnt_copy(i).start()

        if t == CSTEP:
            for i in range(1, 4):
                cnt_wait(i)
            cnt_half[0] = cnt_line[0] + cnt_line[1] + cnt_line[2] + cnt_line[3]
            half_copy.start()

        if t == QSTEP:
            zq_copy.wait_recv()
            q_all[xy] = (
                    zq_out[...].astype(F32) * jnp.exp2(plane_log - full_log)
                    + zq_in[...].astype(F32) * jnp.exp2(zstat_in[0] - full_log)).astype(BF16)
            each(lambda i: qa_copy(i).start())

    for q in range(SUBS):
        @pl.when(place > 0)
        def _():
            in_copy(last - 1, q).wait_recv()
            own[share(place), sub(q)] += in_in[last - 1, :, sub(q)].astype(F32)

        @pl.when(place < 3)
        def _():
            out_copy(2, q).wait_recv()
            own[share(place), sub(q)] += out_in[2, :, sub(q)].astype(F32)

        sums_ref[part, :, sub(q)] = own[share(place), sub(q)]

    for q in range(SUBS):
        pltpu.make_async_remote_copy(
            direct_in.at[:, sub(q)], direct_in.at[:, sub(q)], in_s.at[0, q], direct_r.at[q],
            device_id=partner, device_id_type=MESH).wait_recv()
        sums_ref[1 - part, :, sub(q)] = direct_in[:, sub(q)].astype(F32)

    half_copy.wait_recv()
    counts_ref[part] = cnt_half[0]
    counts_ref[1 - part] = cnt_half[1]
    each(qa_wait)
    quant_ref[...] = q_all[...]

    strip_copy.wait_send()
    each(lambda i: spread_copy(i).wait_send())
    each(lambda i: stat_copy(i).wait_send())
    each(lambda i: q_copy(i).wait_send())
    each(lambda i: qa_copy(i).wait_send())
    for k in range(3):
        zstat_copy(k).wait_send()
    zq_copy.wait_send()
    cntp_copy.wait_send()
    for i in range(1, 4):
        cnt_copy(i).wait_send()
    half_copy.wait_send()
    for q in range(SUBS):
        pair_copy(q).wait_send()
    for t in range(last):
        @pl.when(t >= place)
        def _():
            for q in range(SUBS):
                in_copy(t, q).wait_send()

        if t < 3:
            @pl.when((place > 0) & (t >= 3 - place))
            def _():
                for q in range(SUBS):
                    out_copy(t, q).wait_send()


def finish(quant_t_ref, counts_ref, sums_ref, old_counts_ref, old_sums_ref, quant_ref, counts_next_ref, next_ref):
    quant_ref[...] = quant_t_ref[...].reshape(WIDTH, ROWS).T
    for half in range(2):
        codes = pl.ds(half * PART, PART)
        counts_next = 0.9 * old_counts_ref[:, codes] + 0.1 * counts_ref[half]
        counts_next_ref[:, codes] = counts_next
        next_ref[:, codes] = (0.9 * old_sums_ref[:, codes] + 0.1 * sums_ref[half]) / counts_next


def body(latents, codebook, old_counts, old_sums):
    any_spec = pl.BlockSpec(memory_space=pl.ANY)
    vmem_spec = pl.BlockSpec(memory_space=pltpu.VMEM)
    dma = pltpu.SemaphoreType.DMA
    quant_t, counts, code_sums = pl.pallas_call(
        kernel,
        out_shape=(
            jax.ShapeDtypeStruct((PLANE, PIECE, ROWS), BF16),
            jax.ShapeDtypeStruct((2, 1, PART), F32),
            jax.ShapeDtypeStruct((2, SHARE, PART), F32),
        ),
        in_specs=[any_spec, any_spec],
        out_specs=(vmem_spec, vmem_spec, vmem_spec),
        scratch_shapes=[
            pltpu.VMEM((ROWS, WIDTH), BF16),
            pltpu.VMEM((WIDTH, ROWS), BF16),
            pltpu.VMEM((ROWS, WIDTH), BF16),
            pltpu.VMEM((WIDTH, ROWS), BF16),
            pltpu.VMEM((CODES, WIDTH), BF16),
            pltpu.VMEM((WIDTH, CODES), BF16),
            pltpu.VMEM((CODES, ROWS), F32),
            pltpu.VMEM((CODES, ROWS), BF16),
            pltpu.VMEM((PART, ROWS), BF16),
            pltpu.VMEM((PLANE, 1, ROWS), F32),
            pltpu.VMEM((1, ROWS), F32),
            pltpu.VMEM((3, 1, ROWS), F32),
            pltpu.VMEM((WIDTH, ROWS), BF16),
            pltpu.VMEM((PLANE, PIECE, ROWS), BF16),
            pltpu.VMEM((PIECE, ROWS), BF16),
            pltpu.VMEM((PIECE, ROWS), BF16),
            pltpu.VMEM((PLANE, PIECE, ROWS), BF16),
            pltpu.VMEM((WIDTH + SHARE, ROWS), BF16),
            pltpu.VMEM((WIDTH + SHARE, ROWS), BF16),
            pltpu.VMEM((HALF, PART), F32),
            pltpu.VMEM((HALF, PART), BF16),
            pltpu.VMEM((HALF, PART), BF16),
            pltpu.VMEM((1, PART), F32),
            pltpu.VMEM((1, PART), F32),
            pltpu.VMEM((4, 1, PART), F32),
            pltpu.VMEM((2, 1, PART), F32),
            pltpu.VMEM((LINE - 1, SHARE, PART), BF16),
            pltpu.VMEM((LINE - 1, SHARE, PART), BF16),
            pltpu.VMEM((3, SHARE, PART), BF16),
            pltpu.VMEM((3, SHARE, PART), BF16),
            pltpu.VMEM((SHARE, PART), BF16),
            dma,
            dma((BLOCKS,)),
            dma,
            dma,
            dma((PLANE,)),
            dma((PLANE,)),
            dma((PLANE,)),
            dma((PLANE,)),
            dma((3,)),
            dma((3,)),
            dma((PLANE,)),
            dma((PLANE,)),
            dma((2,)),
            dma((PLANE,)),
            dma((PLANE,)),
            dma((SUBS,)),
            dma((SUBS,)),
            dma((2,)),
            dma((4,)),
            dma((4,)),
            dma((2,)),
            dma((LINE - 1, SUBS)),
            dma((LINE - 1, SUBS)),
            dma((3, SUBS)),
            dma((3, SUBS)),
            dma((SUBS,)),
            pltpu.SemaphoreType.REGULAR,
        ],
        compiler_params=pltpu.CompilerParams(
            collective_id=0, has_side_effects=True, vmem_limit_bytes=60 * 1024 * 1024),
        cost_estimate=pl.CostEstimate(flops=6_500_000_000, bytes_accessed=4_000_000, transcendentals=4_200_000),
    )(latents, codebook)
    quantized, counts_next, codebook_next = pl.pallas_call(
        finish,
        out_shape=(
            jax.ShapeDtypeStruct((ROWS, WIDTH), BF16),
            jax.ShapeDtypeStruct((1, CODES), F32),
            jax.ShapeDtypeStruct((SHARE, CODES), F32),
        ),
        in_specs=[vmem_spec] * 5,
        out_specs=(vmem_spec, vmem_spec, vmem_spec),
        cost_estimate=pl.CostEstimate(flops=300_000, bytes_accessed=2_000_000, transcendentals=0),
    )(quant_t, counts, code_sums, old_counts.reshape(1, CODES), old_sums)
    return quantized, counts_next.reshape(CODES), codebook_next


def solution(mesh):
    return jax.shard_map(
        body,
        mesh=mesh,
        in_specs=(P("dp", None), P("code", None), P("code"), P("dp", "code")),
        out_specs=(P("dp", None), P("code"), P("dp", "code")),
        check_vma=False,
    )
```

```python
import math

import jax
import jax.numpy as jnp
from jax import lax
from jax.experimental import pallas as pl
from jax.experimental.pallas import tpu as pltpu
from jax.sharding import PartitionSpec as P

MESH = pl.DeviceIdType.MESH
F32 = jnp.float32
BF16 = jnp.bfloat16

ROWS = 1024
CODES = 4096
WIDTH = 256
BLOCK = 2048
BLOCKS = CODES // BLOCK
PLANE = 16
GROUP = ROWS // 4
STRIP = ROWS // PLANE
PIECE = WIDTH // PLANE
LINE = 8
PART = CODES // 2
SUBS = 2
SUB = PART // SUBS
SHARE = 16
HALF = SHARE * LINE
GSTEP = 1


def dot(a, b):
    return lax.dot_general(a, b, (((1,), (0,)), ((), ())), preferred_element_type=F32)


def dot_t(a, b):
    return lax.dot_general(a, b, (((1,), (1,)), ((), ())), preferred_element_type=F32)


def kernel(
    latents_hbm, codebook_hbm, quant_ref, counts_ref, sums_ref,
    lat, lat_t, lat2, lat2_t, code, code_t, logits, raised, raised2,
    stat_in, zstat_out, zstat_in,
    q_send, q_in, zq_out, zq_in, q_all,
    norms2, top2_ref, scaled, scaled2, own, pair_out, pair_in, cnt, cnt_pair, cnt_line, cnt_half,
    in_in, in_out, out_in, out_out, direct_in,
    lat_sem, code_sem, strip_s, strip_r, spread_s, spread_r,
    stat_s, stat_r, zstat_s, zstat_r, q_s, q_r, zq_sem, qa_s, qa_r,
    pair_s, pair_r, cntp_sem, cnt_s, cnt_r, half_sem, in_s, in_r, out_s, out_r, direct_r, ready,
):
    dp = lax.axis_index("dp")
    cd = lax.axis_index("code")
    z = dp // 2
    core = dp % 2
    zh = cd // PLANE
    xy = cd % PLANE
    partner = (dp + 1 - 2 * core, cd)
    cd_across = (1 - zh) * PLANE + xy
    across = (dp, cd_across)
    dp_pair = (dp + LINE) % (2 * LINE)
    part = z // 4
    place = z + part * (7 - 2 * z)
    relatives = (across, (dp_pair, cd), (dp_pair, cd_across))

    middle = ((4 - part) * 2 + core, cd)

    def mate(i):
        return ((part * 4 + (z + i) % 4) * 2 + core, cd)

    def peer(i):
        j = (xy + i) % PLANE
        return j, (dp, zh * PLANE + j)

    lat_copy = pltpu.make_async_copy(latents_hbm, lat, lat_sem)
    lat_copy.start()

    def code_copy(b):
        rows = pl.ds(pl.multiple_of(b * BLOCK, BLOCK), BLOCK)
        return pltpu.make_async_copy(codebook_hbm.at[rows], code.at[rows], code_sem.at[b])

    for b in range(BLOCKS):
        code_copy(b).start()

    barrier = pltpu.get_barrier_semaphore()

    def greet(i, carry):
        pl.semaphore_signal(barrier, inc=1, device_id=peer(i)[1], device_id_type=MESH)
        return carry

    lax.fori_loop(1, PLANE, greet, 0)
    greeted = [partner, (dp_pair, cd)] + [mate(i) for i in (1, 2, 3)]
    for device in greeted:
        pl.semaphore_signal(barrier, inc=1, device_id=device, device_id_type=MESH)

    @pl.when(place > 0)
    def _():
        pl.semaphore_signal(barrier, inc=1, device_id=middle, device_id_type=MESH)

    @pl.when(zh == 0)
    def _():
        for device in (across, (dp_pair, cd_across)):
            pl.semaphore_signal(barrier, inc=1, device_id=device, device_id_type=MESH)

    lat_copy.wait()
    lat_t[...] = lat[...].T
    per_dot = 2.0 * 2.0 / math.sqrt(WIDTH) * math.log2(math.e)
    per_norm = 2.0 / math.sqrt(WIDTH) * math.log2(math.e)

    def first(b, top):
        code_copy(b).wait()
        rows = pl.ds(pl.multiple_of(b * BLOCK, BLOCK), BLOCK)
        block = code[rows, :]
        wide = block.astype(F32)
        norms = jnp.sum(wide * wide, axis=1, keepdims=True) * per_norm
        part = dot(block, lat_t[...]) * per_dot - norms
        logits[rows, :] = part
        code_t[:, rows] = block.T
        return jnp.maximum(top, jnp.max(part.reshape(BLOCK // 8, 8, ROWS), axis=0))

    top = lax.fori_loop(0, BLOCKS, first, jnp.full((8, ROWS), -jnp.inf, F32))
    top = jnp.max(top, axis=0, keepdims=True)

    near = PLANE - 1 + 2 + 3
    for side in range(2):
        for mid in range(2):
            @pl.when((zh == side) & ((place == 3) == (mid == 1)))
            def _():
                pl.semaphore_wait(barrier, near + 2 * side + 3 * mid)

    @pl.when(zh == 1)
    def _():
        for device in (across, (dp_pair, cd_across)):
            pl.semaphore_signal(ready, inc=1, device_id=device, device_id_type=MESH)

    def strip(j):
        return pl.ds(pl.multiple_of(j * STRIP, STRIP), STRIP)

    strip_copy = pltpu.make_async_remote_copy(
        lat.at[strip(xy)], lat2.at[strip(xy)], strip_s, strip_r, device_id=(dp_pair, cd), device_id_type=MESH)
    strip_copy.start()

    def second(b, total):
        rows = pl.ds(pl.multiple_of(b * BLOCK, BLOCK), BLOCK)
        part = jnp.exp2(logits[rows, :] - top)
        low = part.astype(BF16)
        raised[rows, :] = low
        return total + jnp.sum(part.reshape(BLOCK // 8, 8, ROWS), axis=0)

    total = lax.fori_loop(0, BLOCKS, second, jnp.zeros((8, ROWS), F32))
    total = jnp.sum(total, axis=0, keepdims=True)

    stat_in[xy] = top + jnp.log2(total)
    def stat_copy(i):
        j, device = peer(i)
        return pltpu.make_async_remote_copy(
            stat_in.at[xy], stat_in.at[xy], stat_s.at[i], stat_r.at[xy], device_id=device, device_id_type=MESH)

    def stat_wait(i):
        j, device = peer(i)
        pltpu.make_async_remote_copy(
            stat_in.at[j], stat_in.at[j], stat_s.at[i], stat_r.at[j], device_id=device, device_id_type=MESH).wait_recv()

    def each(run):
        def step(i, carry):
            run(i)
            return carry
        lax.fori_loop(1, PLANE, step, 0)

    each(lambda i: stat_copy(i).start())

    q_send[...] = (dot(code_t[...], raised[...]) * (1.0 / total)).astype(BF16)

    def piece(j):
        return pl.ds(pl.multiple_of(j * PIECE, PIECE), PIECE)

    def q_copy(i):
        j, device = peer(i)
        return pltpu.make_async_remote_copy(
            q_send.at[piece(j)], q_in.at[xy], q_s.at[i], q_r.at[xy], device_id=device, device_id_type=MESH)

    def q_wait(i):
        j, device = peer(i)
        pltpu.make_async_remote_copy(
            q_send.at[piece(j)], q_in.at[j], q_s.at[i], q_r.at[j], device_id=device, device_id_type=MESH).wait_recv()

    def spread_copy(i):
        j, device = peer(i)
        return pltpu.make_async_remote_copy(
            lat2.at[strip(xy)], lat2.at[strip(xy)], spread_s.at[i], spread_r.at[xy], device_id=device, device_id_type=MESH)

    strip_copy.wait_recv()
    each(lambda i: spread_copy(i).start())
    @pl.when(core == 0)
    def _():
        each(lambda i: q_copy(i).start())


    q_in[xy] = q_send[piece(xy), :]

    each(stat_wait)
    plane_top = stat_in[0]
    for j in range(1, PLANE):
        plane_top = jnp.maximum(plane_top, stat_in[j])
    plane_total = jnp.zeros((1, ROWS), F32)
    for j in range(PLANE):
        plane_total += jnp.exp2(stat_in[j] - plane_top)
    plane_log = plane_top + jnp.log2(plane_total)
    zstat_out[...] = plane_log

    def zstat_copy(k):
        return pltpu.make_async_remote_copy(
            zstat_out, zstat_in.at[k], zstat_s.at[k], zstat_r.at[k], device_id=relatives[k], device_id_type=MESH)

    @pl.when(zh == 0)
    def _():
        pl.semaphore_wait(ready, 2)

    for k in range(3):
        zstat_copy(k).start()

    start = pl.multiple_of(part * PART, PART)
    wide = code[pl.ds(start, PART), :].astype(F32)
    norms2[...] = jnp.sum(wide * wide, axis=1, keepdims=True) * per_norm

    def again(g, carry):
        group = (xy // 4 + g) % 4

        def arrive(i, carry):
            j = group * 4 + i

            @pl.when(j != xy)
            def _():
                pltpu.make_async_remote_copy(
                    lat2.at[strip(j)], lat2.at[strip(j)], spread_s.at[i], spread_r.at[j],
                    device_id=partner, device_id_type=MESH).wait_recv()
            return carry

        lax.fori_loop(0, 4, arrive, 0)
        some = pl.ds(pl.multiple_of(group * GROUP, GROUP), GROUP)
        lat2_t[:, some] = lat2[some, :].T
        logits2 = dot(code[pl.ds(start, PART), :], lat2_t[:, some]) * per_dot - norms2[...]
        logits[0:PART, 0:GROUP] = logits2
        high = jnp.max(jnp.max(logits2.reshape(PART // 8, 8, GROUP), axis=0), axis=0, keepdims=True)
        top2_ref[:, some] = high
        raised2[:, some] = jnp.exp2(logits[0:PART, 0:GROUP] - high).astype(BF16)

        @pl.when((core == 1) & (g == GSTEP))
        def _():
            each(lambda i: q_copy(i).start())

        return carry

    lax.fori_loop(0, 4, again, 0)
    top2 = top2_ref[...]

    def log_sum(a, b):
        high = jnp.maximum(a, b)
        return high + jnp.log2(jnp.exp2(a - high) + jnp.exp2(b - high))

    for k in range(3):
        zstat_copy(k).wait_recv()
    full_log = log_sum(plane_log, zstat_in[0])
    factor = jnp.exp2(top - full_log)
    factor2 = jnp.exp2(top2 - log_sum(zstat_in[1], zstat_in[2]))

    line_no = lax.broadcasted_iota(jnp.int32, (SHARE, ROWS), 0)
    for out, rows_t, by in ((scaled, lat_t, factor), (scaled2, lat2_t, factor2)):
        for side in range(2):
            which = core if side == 0 else 1 - core
            for e in range(LINE):
                chip = e + part * (LINE - 1 - 2 * e)
                src = pl.ds(pl.multiple_of(chip * 2 * SHARE + which * SHARE, SHARE), SHARE)
                out[side * HALF + e * SHARE : side * HALF + (e + 1) * SHARE, :] = (
                    rows_t[src, :].astype(F32) * by).astype(BF16)
        high = by.astype(BF16).astype(F32)
        out[WIDTH : WIDTH + SHARE, :] = jnp.where(
            line_no == 0, high, jnp.where(line_no == 1, by - high, 0.0)).astype(BF16)

    def sub(q):
        return pl.ds(q * SUB, SUB)

    def pair_copy(q):
        return pltpu.make_async_remote_copy(
            pair_out.at[:, sub(q)], pair_in.at[:, sub(q)], pair_s.at[q], pair_r.at[q],
            device_id=partner, device_id_type=MESH)

    for q in range(SUBS):
        mine = pl.ds(pl.multiple_of(part * PART + q * SUB, SUB), SUB)
        sums = dot_t(scaled[...], raised[mine, :]) + dot_t(scaled2[...], raised2[sub(q), :])
        pair_out[:, sub(q)] = sums[HALF:WIDTH].astype(BF16)
        pair_copy(q).start()
        own[:, sub(q)] = sums[0:HALF]
        cnt[:, sub(q)] = sums[WIDTH : WIDTH + 1] + sums[WIDTH + 1 : WIDTH + 2]

    cntp_copy = pltpu.make_async_remote_copy(
        cnt, cnt_pair, cntp_sem.at[0], cntp_sem.at[1], device_id=partner, device_id_type=MESH)
    cntp_copy.start()

    each(q_wait)
    plane_q = jnp.zeros((PIECE, ROWS), F32)
    for j in range(PLANE):
        plane_q += q_in[j].astype(F32) * jnp.exp2(stat_in[j] - plane_log)
    zq_out[...] = plane_q.astype(BF16)
    zq_copy = pltpu.make_async_remote_copy(
        zq_out, zq_in, zq_sem.at[0], zq_sem.at[1], device_id=across, device_id_type=MESH)
    zq_copy.start()

    toward = 2 * (1 - 2 * part)
    last = LINE - 1

    def in_copy(t, q):
        return pltpu.make_async_remote_copy(
            in_out.at[t, :, sub(q)], in_in.at[t, :, sub(q)], in_s.at[t, q], in_r.at[t, q],
            device_id=(dp + toward, cd), device_id_type=MESH)

    def direct_copy(t, q):
        e = 10 - t
        chip = e + part * (last - 2 * e)
        return pltpu.make_async_remote_copy(
            in_out.at[t, :, sub(q)], direct_in.at[:, sub(q)], in_s.at[t, q], direct_r.at[q],
            device_id=(chip * 2 + core, cd), device_id_type=MESH)

    def out_copy(t, q):
        return pltpu.make_async_remote_copy(
            out_out.at[t, :, sub(q)], out_in.at[t, :, sub(q)], out_s.at[t, q], out_r.at[t, q],
            device_id=(dp - toward, cd), device_id_type=MESH)

    def share(e):
        return pl.ds(pl.multiple_of(e * SHARE, SHARE), SHARE)

    def in_step(t, q):
        @pl.when(t >= place)
        def _():
            mine = own[share(last - t + place), sub(q)]

            @pl.when(place == 0)
            def _():
                in_out[t, :, sub(q)] = mine.astype(BF16)

            if t > 0:
                @pl.when(place > 0)
                def _():
                    in_copy(t - 1, q).wait_recv()
                    in_out[t, :, sub(q)] = (mine + in_in[t - 1, :, sub(q)].astype(F32)).astype(BF16)

            @pl.when(place < 3)
            def _():
                in_copy(t, q).start()

            if t >= 3:
                @pl.when(place == 3)
                def _():
                    direct_copy(t, q).start()

    def out_step(t, q):
        @pl.when((place > 0) & (t >= 3 - place))
        def _():
            mine = own[share(t - 3 + place), sub(q)]

            @pl.when(place == 3)
            def _():
                out_out[t, :, sub(q)] = mine.astype(BF16)

            if t > 0:
                @pl.when(place < 3)
                def _():
                    out_copy(t - 1, q).wait_recv()
                    out_out[t, :, sub(q)] = (mine + out_in[t - 1, :, sub(q)].astype(F32)).astype(BF16)

            out_copy(t, q).start()

    def cnt_copy(i):
        return pltpu.make_async_remote_copy(
            cnt_line.at[z % 4], cnt_line.at[z % 4], cnt_s.at[i], cnt_r.at[z % 4], device_id=mate(i), device_id_type=MESH)

    def cnt_wait(i):
        other = (z + i) % 4
        pltpu.make_async_remote_copy(
            cnt_line.at[other], cnt_line.at[other], cnt_s.at[i], cnt_r.at[other],
            device_id=mate(i), device_id_type=MESH).wait_recv()

    half_copy = pltpu.make_async_remote_copy(
        cnt_half.at[0], cnt_half.at[1], half_sem.at[0], half_sem.at[1], device_id=(dp_pair, cd), device_id_type=MESH)

    def qa_copy(i):
        j, device = peer(i)
        return pltpu.make_async_remote_copy(
            q_all.at[xy], q_all.at[xy], qa_s.at[i], qa_r.at[xy], device_id=device, device_id_type=MESH)

    def qa_wait(i):
        j, device = peer(i)
        pltpu.make_async_remote_copy(
            q_all.at[j], q_all.at[j], qa_s.at[i], qa_r.at[j], device_id=device, device_id_type=MESH).wait_recv()

    for t in range(last):
        for q in range(SUBS):
            if t == 0:
                pair_copy(q).wait_recv()
                own[:, sub(q)] += pair_in[:, sub(q)].astype(F32)
            in_step(t, q)
            if t < 3:
                out_step(t, q)
        if t == 0:
            cntp_copy.wait_recv()
            cnt_line[z % 4] = cnt_pair[...] + cnt[...]

            for i in range(1, 4):
                cnt_copy(i).start()

        if t in (2, last - 1):
            @pl.when((place == 0) == (t == last - 1))
            def _():
                for i in range(1, 4):
                    cnt_wait(i)
                cnt_half[0] = cnt_line[0] + cnt_line[1] + cnt_line[2] + cnt_line[3]
                half_copy.start()

                zq_copy.wait_recv()
                q_all[xy] = (
                        zq_out[...].astype(F32) * jnp.exp2(plane_log - full_log)
                        + zq_in[...].astype(F32) * jnp.exp2(zstat_in[0] - full_log)).astype(BF16)
                each(lambda i: qa_copy(i).start())

    for q in range(SUBS):
        @pl.when(place > 0)
        def _():
            in_copy(last - 1, q).wait_recv()
            own[share(place), sub(q)] += in_in[last - 1, :, sub(q)].astype(F32)

        @pl.when(place < 3)
        def _():
            out_copy(2, q).wait_recv()
            own[share(place), sub(q)] += out_in[2, :, sub(q)].astype(F32)

        sums_ref[part, :, sub(q)] = own[share(place), sub(q)]

    for q in range(SUBS):
        pltpu.make_async_remote_copy(
            direct_in.at[:, sub(q)], direct_in.at[:, sub(q)], in_s.at[0, q], direct_r.at[q],
            device_id=partner, device_id_type=MESH).wait_recv()
        sums_ref[1 - part, :, sub(q)] = direct_in[:, sub(q)].astype(F32)

    half_copy.wait_recv()
    counts_ref[part] = cnt_half[0]
    counts_ref[1 - part] = cnt_half[1]
    each(qa_wait)
    quant_ref[...] = q_all[...]

    strip_copy.wait_send()
    each(lambda i: spread_copy(i).wait_send())
    each(lambda i: stat_copy(i).wait_send())
    each(lambda i: q_copy(i).wait_send())
    each(lambda i: qa_copy(i).wait_send())
    for k in range(3):
        zstat_copy(k).wait_send()
    zq_copy.wait_send()
    cntp_copy.wait_send()
    for i in range(1, 4):
        cnt_copy(i).wait_send()
    half_copy.wait_send()
    for q in range(SUBS):
        pair_copy(q).wait_send()
    for t in range(last):
        @pl.when(t >= place)
        def _():
            for q in range(SUBS):
                in_copy(t, q).wait_send()

        if t < 3:
            @pl.when((place > 0) & (t >= 3 - place))
            def _():
                for q in range(SUBS):
                    out_copy(t, q).wait_send()


def finish(quant_t_ref, counts_ref, sums_ref, old_counts_ref, old_sums_ref, quant_ref, counts_next_ref, next_ref):
    quant_ref[...] = quant_t_ref[...].reshape(WIDTH, ROWS).T
    for half in range(2):
        codes = pl.ds(half * PART, PART)
        counts_next = 0.9 * old_counts_ref[:, codes] + 0.1 * counts_ref[half]
        counts_next_ref[:, codes] = counts_next
        next_ref[:, codes] = (0.9 * old_sums_ref[:, codes] + 0.1 * sums_ref[half]) / counts_next


def body(latents, codebook, old_counts, old_sums):
    any_spec = pl.BlockSpec(memory_space=pl.ANY)
    vmem_spec = pl.BlockSpec(memory_space=pltpu.VMEM)
    dma = pltpu.SemaphoreType.DMA
    quant_t, counts, code_sums = pl.pallas_call(
        kernel,
        out_shape=(
            jax.ShapeDtypeStruct((PLANE, PIECE, ROWS), BF16),
            jax.ShapeDtypeStruct((2, 1, PART), F32),
            jax.ShapeDtypeStruct((2, SHARE, PART), F32),
        ),
        in_specs=[any_spec, any_spec],
        out_specs=(vmem_spec, vmem_spec, vmem_spec),
        scratch_shapes=[
            pltpu.VMEM((ROWS, WIDTH), BF16),
            pltpu.VMEM((WIDTH, ROWS), BF16),
            pltpu.VMEM((ROWS, WIDTH), BF16),
            pltpu.VMEM((WIDTH, ROWS), BF16),
            pltpu.VMEM((CODES, WIDTH), BF16),
            pltpu.VMEM((WIDTH, CODES), BF16),
            pltpu.VMEM((CODES, ROWS), F32),
            pltpu.VMEM((CODES, ROWS), BF16),
            pltpu.VMEM((PART, ROWS), BF16),
            pltpu.VMEM((PLANE, 1, ROWS), F32),
            pltpu.VMEM((1, ROWS), F32),
            pltpu.VMEM((3, 1, ROWS), F32),
            pltpu.VMEM((WIDTH, ROWS), BF16),
            pltpu.VMEM((PLANE, PIECE, ROWS), BF16),
            pltpu.VMEM((PIECE, ROWS), BF16),
            pltpu.VMEM((PIECE, ROWS), BF16),
            pltpu.VMEM((PLANE, PIECE, ROWS), BF16),
            pltpu.VMEM((PART, 1), F32),
            pltpu.VMEM((1, ROWS), F32),
            pltpu.VMEM((WIDTH + SHARE, ROWS), BF16),
            pltpu.VMEM((WIDTH + SHARE, ROWS), BF16),
            pltpu.VMEM((HALF, PART), F32),
            pltpu.VMEM((HALF, PART), BF16),
            pltpu.VMEM((HALF, PART), BF16),
            pltpu.VMEM((1, PART), F32),
            pltpu.VMEM((1, PART), F32),
            pltpu.VMEM((4, 1, PART), F32),
            pltpu.VMEM((2, 1, PART), F32),
            pltpu.VMEM((LINE - 1, SHARE, PART), BF16),
            pltpu.VMEM((LINE - 1, SHARE, PART), BF16),
            pltpu.VMEM((3, SHARE, PART), BF16),
            pltpu.VMEM((3, SHARE, PART), BF16),
            pltpu.VMEM((SHARE, PART), BF16),
            dma,
            dma((BLOCKS,)),
            dma,
            dma,
            dma((PLANE,)),
            dma((PLANE,)),
            dma((PLANE,)),
            dma((PLANE,)),
            dma((3,)),
            dma((3,)),
            dma((PLANE,)),
            dma((PLANE,)),
            dma((2,)),
            dma((PLANE,)),
            dma((PLANE,)),
            dma((SUBS,)),
            dma((SUBS,)),
            dma((2,)),
            dma((4,)),
            dma((4,)),
            dma((2,)),
            dma((LINE - 1, SUBS)),
            dma((LINE - 1, SUBS)),
            dma((3, SUBS)),
            dma((3, SUBS)),
            dma((SUBS,)),
            pltpu.SemaphoreType.REGULAR,
        ],
        compiler_params=pltpu.CompilerParams(
            collective_id=0, has_side_effects=True, vmem_limit_bytes=60 * 1024 * 1024),
        cost_estimate=pl.CostEstimate(flops=6_500_000_000, bytes_accessed=4_000_000, transcendentals=4_200_000),
    )(latents, codebook)
    quantized, counts_next, codebook_next = pl.pallas_call(
        finish,
        out_shape=(
            jax.ShapeDtypeStruct((ROWS, WIDTH), BF16),
            jax.ShapeDtypeStruct((1, CODES), F32),
            jax.ShapeDtypeStruct((SHARE, CODES), F32),
        ),
        in_specs=[vmem_spec] * 5,
        out_specs=(vmem_spec, vmem_spec, vmem_spec),
        cost_estimate=pl.CostEstimate(flops=300_000, bytes_accessed=2_000_000, transcendentals=0),
    )(quant_t, counts, code_sums, old_counts.reshape(1, CODES), old_sums)
    return quantized, counts_next.reshape(CODES), codebook_next


def solution(mesh):
    return jax.shard_map(
        body,
        mesh=mesh,
        in_specs=(P("dp", None), P("code", None), P("code"), P("dp", "code")),
        out_specs=(P("dp", None), P("code"), P("dp", "code")),
        check_vma=False,
    )
```

```python
import math

import jax
import jax.numpy as jnp
from jax import lax
from jax.experimental import pallas as pl
from jax.experimental.pallas import tpu as pltpu
from jax.sharding import PartitionSpec as P

MESH = pl.DeviceIdType.MESH
F32 = jnp.float32
BF16 = jnp.bfloat16

ROWS = 1024
CODES = 4096
WIDTH = 256
BLOCK = 2048
BLOCKS = CODES // BLOCK
PLANE = 16
GROUP = ROWS // 4
STRIP = ROWS // PLANE
PIECE = WIDTH // PLANE
LINE = 8
PART = CODES // 2
SUBS = 4
SUB = PART // SUBS
SHARE = 16
HALF = SHARE * LINE
GSTEP = 1


def dot(a, b):
    return lax.dot_general(a, b, (((1,), (0,)), ((), ())), preferred_element_type=F32)


def dot_t(a, b):
    return lax.dot_general(a, b, (((1,), (1,)), ((), ())), preferred_element_type=F32)


def kernel(
    latents_hbm, codebook_hbm, quant_ref, counts_ref, sums_ref,
    lat, lat_t, lat2, lat2_t, code, code_t, logits, raised, raised2,
    stat_in, zstat_out, zstat_in,
    q_send, q_in, zq_out, zq_in, q_all,
    norms2, top2_ref, scaled, scaled2, own, pair_out, pair_in, cnt, cnt_pair, cnt_line, cnt_half,
    in_in, in_out, out_in, out_out, direct_in,
    lat_sem, code_sem, strip_s, strip_r, spread_s, spread_r,
    stat_s, stat_r, zstat_s, zstat_r, q_s, q_r, zq_sem, qa_s, qa_r,
    pair_s, pair_r, cntp_sem, cnt_s, cnt_r, half_sem, in_s, in_r, out_s, out_r, direct_r, ready,
):
    dp = lax.axis_index("dp")
    cd = lax.axis_index("code")
    z = dp // 2
    core = dp % 2
    zh = cd // PLANE
    xy = cd % PLANE
    partner = (dp + 1 - 2 * core, cd)
    cd_across = (1 - zh) * PLANE + xy
    across = (dp, cd_across)
    dp_pair = (dp + LINE) % (2 * LINE)
    part = z // 4
    place = z + part * (7 - 2 * z)
    relatives = (across, (dp_pair, cd), (dp_pair, cd_across))

    middle = ((4 - part) * 2 + core, cd)

    def mate(i):
        return ((part * 4 + (z + i) % 4) * 2 + core, cd)

    def peer(i):
        j = (xy + i) % PLANE
        return j, (dp, zh * PLANE + j)

    lat_copy = pltpu.make_async_copy(latents_hbm, lat, lat_sem)
    lat_copy.start()

    def code_copy(b):
        rows = pl.ds(pl.multiple_of(b * BLOCK, BLOCK), BLOCK)
        return pltpu.make_async_copy(codebook_hbm.at[rows], code.at[rows], code_sem.at[b])

    for b in range(BLOCKS):
        code_copy(b).start()

    barrier = pltpu.get_barrier_semaphore()

    def greet(i, carry):
        pl.semaphore_signal(barrier, inc=1, device_id=peer(i)[1], device_id_type=MESH)
        return carry

    lax.fori_loop(1, PLANE, greet, 0)
    greeted = [partner, (dp_pair, cd)] + [mate(i) for i in (1, 2, 3)]
    for device in greeted:
        pl.semaphore_signal(barrier, inc=1, device_id=device, device_id_type=MESH)

    @pl.when(place > 0)
    def _():
        pl.semaphore_signal(barrier, inc=1, device_id=middle, device_id_type=MESH)

    @pl.when(zh == 0)
    def _():
        for device in (across, (dp_pair, cd_across)):
            pl.semaphore_signal(barrier, inc=1, device_id=device, device_id_type=MESH)

    lat_copy.wait()
    lat_t[...] = lat[...].T
    per_dot = 2.0 * 2.0 / math.sqrt(WIDTH) * math.log2(math.e)
    per_norm = 2.0 / math.sqrt(WIDTH) * math.log2(math.e)

    def first(b, top):
        code_copy(b).wait()
        rows = pl.ds(pl.multiple_of(b * BLOCK, BLOCK), BLOCK)
        block = code[rows, :]
        wide = block.astype(F32)
        norms = jnp.sum(wide * wide, axis=1, keepdims=True) * per_norm
        part = dot(block, lat_t[...]) * per_dot - norms
        logits[rows, :] = part
        code_t[:, rows] = block.T
        return jnp.maximum(top, jnp.max(part.reshape(BLOCK // 8, 8, ROWS), axis=0))

    top = lax.fori_loop(0, BLOCKS, first, jnp.full((8, ROWS), -jnp.inf, F32))
    top = jnp.max(top, axis=0, keepdims=True)

    near = PLANE - 1 + 2 + 3
    for side in range(2):
        for mid in range(2):
            @pl.when((zh == side) & ((place == 3) == (mid == 1)))
            def _():
                pl.semaphore_wait(barrier, near + 2 * side + 3 * mid)

    @pl.when(zh == 1)
    def _():
        for device in (across, (dp_pair, cd_across)):
            pl.semaphore_signal(ready, inc=1, device_id=device, device_id_type=MESH)

    def strip(j):
        return pl.ds(pl.multiple_of(j * STRIP, STRIP), STRIP)

    strip_copy = pltpu.make_async_remote_copy(
        lat.at[strip(xy)], lat2.at[strip(xy)], strip_s, strip_r, device_id=(dp_pair, cd), device_id_type=MESH)
    strip_copy.start()

    def second(b, total):
        rows = pl.ds(pl.multiple_of(b * BLOCK, BLOCK), BLOCK)
        part = jnp.exp2(logits[rows, :] - top)
        low = part.astype(BF16)
        raised[rows, :] = low
        return total + jnp.sum(part.reshape(BLOCK // 8, 8, ROWS), axis=0)

    total = lax.fori_loop(0, BLOCKS, second, jnp.zeros((8, ROWS), F32))
    total = jnp.sum(total, axis=0, keepdims=True)

    stat_in[xy] = top + jnp.log2(total)
    def stat_copy(i):
        j, device = peer(i)
        return pltpu.make_async_remote_copy(
            stat_in.at[xy], stat_in.at[xy], stat_s.at[i], stat_r.at[xy], device_id=device, device_id_type=MESH)

    def stat_wait(i):
        j, device = peer(i)
        pltpu.make_async_remote_copy(
            stat_in.at[j], stat_in.at[j], stat_s.at[i], stat_r.at[j], device_id=device, device_id_type=MESH).wait_recv()

    def each(run):
        def step(i, carry):
            run(i)
            return carry
        lax.fori_loop(1, PLANE, step, 0)

    each(lambda i: stat_copy(i).start())

    q_send[...] = (dot(code_t[...], raised[...]) * (1.0 / total)).astype(BF16)

    def piece(j):
        return pl.ds(pl.multiple_of(j * PIECE, PIECE), PIECE)

    def q_copy(i):
        j, device = peer(i)
        return pltpu.make_async_remote_copy(
            q_send.at[piece(j)], q_in.at[xy], q_s.at[i], q_r.at[xy], device_id=device, device_id_type=MESH)

    def q_wait(i):
        j, device = peer(i)
        pltpu.make_async_remote_copy(
            q_send.at[piece(j)], q_in.at[j], q_s.at[i], q_r.at[j], device_id=device, device_id_type=MESH).wait_recv()

    def spread_copy(i):
        j, device = peer(i)
        return pltpu.make_async_remote_copy(
            lat2.at[strip(xy)], lat2.at[strip(xy)], spread_s.at[i], spread_r.at[xy], device_id=device, device_id_type=MESH)

    strip_copy.wait_recv()
    each(lambda i: spread_copy(i).start())
    @pl.when(core == 0)
    def _():
        each(lambda i: q_copy(i).start())


    q_in[xy] = q_send[piece(xy), :]

    each(stat_wait)
    plane_top = stat_in[0]
    for j in range(1, PLANE):
        plane_top = jnp.maximum(plane_top, stat_in[j])
    plane_total = jnp.zeros((1, ROWS), F32)
    for j in range(PLANE):
        plane_total += jnp.exp2(stat_in[j] - plane_top)
    plane_log = plane_top + jnp.log2(plane_total)
    zstat_out[...] = plane_log

    def zstat_copy(k):
        return pltpu.make_async_remote_copy(
            zstat_out, zstat_in.at[k], zstat_s.at[k], zstat_r.at[k], device_id=relatives[k], device_id_type=MESH)

    @pl.when(zh == 0)
    def _():
        pl.semaphore_wait(ready, 2)

    for k in range(3):
        zstat_copy(k).start()

    start = pl.multiple_of(part * PART, PART)
    wide = code[pl.ds(start, PART), :].astype(F32)
    norms2[...] = jnp.sum(wide * wide, axis=1, keepdims=True) * per_norm

    def again(g, carry):
        group = (xy // 4 + g) % 4

        def arrive(i, carry):
            j = group * 4 + i

            @pl.when(j != xy)
            def _():
                pltpu.make_async_remote_copy(
                    lat2.at[strip(j)], lat2.at[strip(j)], spread_s.at[i], spread_r.at[j],
                    device_id=partner, device_id_type=MESH).wait_recv()
            return carry

        lax.fori_loop(0, 4, arrive, 0)
        some = pl.ds(pl.multiple_of(group * GROUP, GROUP), GROUP)
        lat2_t[:, some] = lat2[some, :].T
        logits2 = dot(code[pl.ds(start, PART), :], lat2_t[:, some]) * per_dot - norms2[...]
        logits[0:PART, 0:GROUP] = logits2
        high = jnp.max(jnp.max(logits2.reshape(PART // 8, 8, GROUP), axis=0), axis=0, keepdims=True)
        top2_ref[:, some] = high
        raised2[:, some] = jnp.exp2(logits[0:PART, 0:GROUP] - high).astype(BF16)

        @pl.when((core == 1) & (g == GSTEP))
        def _():
            each(lambda i: q_copy(i).start())

        return carry

    lax.fori_loop(0, 4, again, 0)
    top2 = top2_ref[...]

    def log_sum(a, b):
        high = jnp.maximum(a, b)
        return high + jnp.log2(jnp.exp2(a - high) + jnp.exp2(b - high))

    for k in range(3):
        zstat_copy(k).wait_recv()
    full_log = log_sum(plane_log, zstat_in[0])
    factor = jnp.exp2(top - full_log)
    factor2 = jnp.exp2(top2 - log_sum(zstat_in[1], zstat_in[2]))

    line_no = lax.broadcasted_iota(jnp.int32, (SHARE, ROWS), 0)
    for out, rows_t, by in ((scaled, lat_t, factor), (scaled2, lat2_t, factor2)):
        for side in range(2):
            which = core if side == 0 else 1 - core
            for e in range(LINE):
                chip = e + part * (LINE - 1 - 2 * e)
                src = pl.ds(pl.multiple_of(chip * 2 * SHARE + which * SHARE, SHARE), SHARE)
                out[side * HALF + e * SHARE : side * HALF + (e + 1) * SHARE, :] = (
                    rows_t[src, :].astype(F32) * by).astype(BF16)
        high = by.astype(BF16).astype(F32)
        out[WIDTH : WIDTH + SHARE, :] = jnp.where(
            line_no == 0, high, jnp.where(line_no == 1, by - high, 0.0)).astype(BF16)

    def sub(q):
        return pl.ds(q * SUB, SUB)

    def pair_copy(q):
        return pltpu.make_async_remote_copy(
            pair_out.at[:, sub(q)], pair_in.at[:, sub(q)], pair_s.at[q], pair_r.at[q],
            device_id=partner, device_id_type=MESH)

    for q in range(SUBS):
        mine = pl.ds(pl.multiple_of(part * PART + q * SUB, SUB), SUB)
        sums = dot_t(scaled[...], raised[mine, :]) + dot_t(scaled2[...], raised2[sub(q), :])
        pair_out[:, sub(q)] = sums[HALF:WIDTH].astype(BF16)
        pair_copy(q).start()
        own[:, sub(q)] = sums[0:HALF]
        cnt[:, sub(q)] = sums[WIDTH : WIDTH + 1] + sums[WIDTH + 1 : WIDTH + 2]

    cntp_copy = pltpu.make_async_remote_copy(
        cnt, cnt_pair, cntp_sem.at[0], cntp_sem.at[1], device_id=partner, device_id_type=MESH)
    cntp_copy.start()

    each(q_wait)
    plane_q = jnp.zeros((PIECE, ROWS), F32)
    for j in range(PLANE):
        plane_q += q_in[j].astype(F32) * jnp.exp2(stat_in[j] - plane_log)
    zq_out[...] = plane_q.astype(BF16)
    zq_copy = pltpu.make_async_remote_copy(
        zq_out, zq_in, zq_sem.at[0], zq_sem.at[1], device_id=across, device_id_type=MESH)
    zq_copy.start()

    toward = 2 * (1 - 2 * part)
    last = LINE - 1

    def in_copy(t, q):
        return pltpu.make_async_remote_copy(
            in_out.at[t, :, sub(q)], in_in.at[t, :, sub(q)], in_s.at[t, q], in_r.at[t, q],
            device_id=(dp + toward, cd), device_id_type=MESH)

    def direct_copy(t, q):
        e = 10 - t
        chip = e + part * (last - 2 * e)
        return pltpu.make_async_remote_copy(
            in_out.at[t, :, sub(q)], direct_in.at[:, sub(q)], in_s.at[t, q], direct_r.at[q],
            device_id=(chip * 2 + core, cd), device_id_type=MESH)

    def out_copy(t, q):
        return pltpu.make_async_remote_copy(
            out_out.at[t, :, sub(q)], out_in.at[t, :, sub(q)], out_s.at[t, q], out_r.at[t, q],
            device_id=(dp - toward, cd), device_id_type=MESH)

    def share(e):
        return pl.ds(pl.multiple_of(e * SHARE, SHARE), SHARE)

    def in_step(t, q):
        @pl.when(t >= place)
        def _():
            mine = own[share(last - t + place), sub(q)]

            @pl.when(place == 0)
            def _():
                in_out[t, :, sub(q)] = mine.astype(BF16)

            if t > 0:
                @pl.when(place > 0)
                def _():
                    in_copy(t - 1, q).wait_recv()
                    in_out[t, :, sub(q)] = (mine + in_in[t - 1, :, sub(q)].astype(F32)).astype(BF16)

            @pl.when(place < 3)
            def _():
                in_copy(t, q).start()

            if t >= 3:
                @pl.when(place == 3)
                def _():
                    direct_copy(t, q).start()

    def out_step(t, q):
        @pl.when((place > 0) & (t >= 3 - place))
        def _():
            mine = own[share(t - 3 + place), sub(q)]

            @pl.when(place == 3)
            def _():
                out_out[t, :, sub(q)] = mine.astype(BF16)

            if t > 0:
                @pl.when(place < 3)
                def _():
                    out_copy(t - 1, q).wait_recv()
                    out_out[t, :, sub(q)] = (mine + out_in[t - 1, :, sub(q)].astype(F32)).astype(BF16)

            out_copy(t, q).start()

    def cnt_copy(i):
        return pltpu.make_async_remote_copy(
            cnt_line.at[z % 4], cnt_line.at[z % 4], cnt_s.at[i], cnt_r.at[z % 4], device_id=mate(i), device_id_type=MESH)

    def cnt_wait(i):
        other = (z + i) % 4
        pltpu.make_async_remote_copy(
            cnt_line.at[other], cnt_line.at[other], cnt_s.at[i], cnt_r.at[other],
            device_id=mate(i), device_id_type=MESH).wait_recv()

    half_copy = pltpu.make_async_remote_copy(
        cnt_half.at[0], cnt_half.at[1], half_sem.at[0], half_sem.at[1], device_id=(dp_pair, cd), device_id_type=MESH)

    def qa_copy(i):
        j, device = peer(i)
        return pltpu.make_async_remote_copy(
            q_all.at[xy], q_all.at[xy], qa_s.at[i], qa_r.at[xy], device_id=device, device_id_type=MESH)

    def qa_wait(i):
        j, device = peer(i)
        pltpu.make_async_remote_copy(
            q_all.at[j], q_all.at[j], qa_s.at[i], qa_r.at[j], device_id=device, device_id_type=MESH).wait_recv()

    for t in range(last):
        for q in range(SUBS):
            if t == 0:
                pair_copy(q).wait_recv()
                own[:, sub(q)] += pair_in[:, sub(q)].astype(F32)
            in_step(t, q)
            if t < 3:
                out_step(t, q)
        if t == 0:
            cntp_copy.wait_recv()
            cnt_line[z % 4] = cnt_pair[...] + cnt[...]

            for i in range(1, 4):
                cnt_copy(i).start()

        if t in (2, last - 1):
            @pl.when((place == 0) == (t == last - 1))
            def _():
                for i in range(1, 4):
                    cnt_wait(i)
                cnt_half[0] = cnt_line[0] + cnt_line[1] + cnt_line[2] + cnt_line[3]
                half_copy.start()

                zq_copy.wait_recv()
                q_all[xy] = (
                        zq_out[...].astype(F32) * jnp.exp2(plane_log - full_log)
                        + zq_in[...].astype(F32) * jnp.exp2(zstat_in[0] - full_log)).astype(BF16)
                each(lambda i: qa_copy(i).start())

    for q in range(SUBS):
        @pl.when(place > 0)
        def _():
            in_copy(last - 1, q).wait_recv()
            own[share(place), sub(q)] += in_in[last - 1, :, sub(q)].astype(F32)

        @pl.when(place < 3)
        def _():
            out_copy(2, q).wait_recv()
            own[share(place), sub(q)] += out_in[2, :, sub(q)].astype(F32)

        sums_ref[part, :, sub(q)] = own[share(place), sub(q)]

    for q in range(SUBS):
        pltpu.make_async_remote_copy(
            direct_in.at[:, sub(q)], direct_in.at[:, sub(q)], in_s.at[0, q], direct_r.at[q],
            device_id=partner, device_id_type=MESH).wait_recv()
        sums_ref[1 - part, :, sub(q)] = direct_in[:, sub(q)].astype(F32)

    half_copy.wait_recv()
    counts_ref[part] = cnt_half[0]
    counts_ref[1 - part] = cnt_half[1]
    each(qa_wait)
    quant_ref[...] = q_all[...]

    strip_copy.wait_send()
    each(lambda i: spread_copy(i).wait_send())
    each(lambda i: stat_copy(i).wait_send())
    each(lambda i: q_copy(i).wait_send())
    each(lambda i: qa_copy(i).wait_send())
    for k in range(3):
        zstat_copy(k).wait_send()
    zq_copy.wait_send()
    cntp_copy.wait_send()
    for i in range(1, 4):
        cnt_copy(i).wait_send()
    half_copy.wait_send()
    for q in range(SUBS):
        pair_copy(q).wait_send()
    for t in range(last):
        @pl.when(t >= place)
        def _():
            for q in range(SUBS):
                in_copy(t, q).wait_send()

        if t < 3:
            @pl.when((place > 0) & (t >= 3 - place))
            def _():
                for q in range(SUBS):
                    out_copy(t, q).wait_send()


def finish(quant_t_ref, counts_ref, sums_ref, old_counts_ref, old_sums_ref, quant_ref, counts_next_ref, next_ref):
    quant_ref[...] = quant_t_ref[...].reshape(WIDTH, ROWS).T
    for half in range(2):
        codes = pl.ds(half * PART, PART)
        counts_next = 0.9 * old_counts_ref[:, codes] + 0.1 * counts_ref[half]
        counts_next_ref[:, codes] = counts_next
        next_ref[:, codes] = (0.9 * old_sums_ref[:, codes] + 0.1 * sums_ref[half]) / counts_next


def body(latents, codebook, old_counts, old_sums):
    any_spec = pl.BlockSpec(memory_space=pl.ANY)
    vmem_spec = pl.BlockSpec(memory_space=pltpu.VMEM)
    dma = pltpu.SemaphoreType.DMA
    quant_t, counts, code_sums = pl.pallas_call(
        kernel,
        out_shape=(
            jax.ShapeDtypeStruct((PLANE, PIECE, ROWS), BF16),
            jax.ShapeDtypeStruct((2, 1, PART), F32),
            jax.ShapeDtypeStruct((2, SHARE, PART), F32),
        ),
        in_specs=[any_spec, any_spec],
        out_specs=(vmem_spec, vmem_spec, vmem_spec),
        scratch_shapes=[
            pltpu.VMEM((ROWS, WIDTH), BF16),
            pltpu.VMEM((WIDTH, ROWS), BF16),
            pltpu.VMEM((ROWS, WIDTH), BF16),
            pltpu.VMEM((WIDTH, ROWS), BF16),
            pltpu.VMEM((CODES, WIDTH), BF16),
            pltpu.VMEM((WIDTH, CODES), BF16),
            pltpu.VMEM((CODES, ROWS), F32),
            pltpu.VMEM((CODES, ROWS), BF16),
            pltpu.VMEM((PART, ROWS), BF16),
            pltpu.VMEM((PLANE, 1, ROWS), F32),
            pltpu.VMEM((1, ROWS), F32),
            pltpu.VMEM((3, 1, ROWS), F32),
            pltpu.VMEM((WIDTH, ROWS), BF16),
            pltpu.VMEM((PLANE, PIECE, ROWS), BF16),
            pltpu.VMEM((PIECE, ROWS), BF16),
            pltpu.VMEM((PIECE, ROWS), BF16),
            pltpu.VMEM((PLANE, PIECE, ROWS), BF16),
            pltpu.VMEM((PART, 1), F32),
            pltpu.VMEM((1, ROWS), F32),
            pltpu.VMEM((WIDTH + SHARE, ROWS), BF16),
            pltpu.VMEM((WIDTH + SHARE, ROWS), BF16),
            pltpu.VMEM((HALF, PART), F32),
            pltpu.VMEM((HALF, PART), BF16),
            pltpu.VMEM((HALF, PART), BF16),
            pltpu.VMEM((1, PART), F32),
            pltpu.VMEM((1, PART), F32),
            pltpu.VMEM((4, 1, PART), F32),
            pltpu.VMEM((2, 1, PART), F32),
            pltpu.VMEM((LINE - 1, SHARE, PART), BF16),
            pltpu.VMEM((LINE - 1, SHARE, PART), BF16),
            pltpu.VMEM((3, SHARE, PART), BF16),
            pltpu.VMEM((3, SHARE, PART), BF16),
            pltpu.VMEM((SHARE, PART), BF16),
            dma,
            dma((BLOCKS,)),
            dma,
            dma,
            dma((PLANE,)),
            dma((PLANE,)),
            dma((PLANE,)),
            dma((PLANE,)),
            dma((3,)),
            dma((3,)),
            dma((PLANE,)),
            dma((PLANE,)),
            dma((2,)),
            dma((PLANE,)),
            dma((PLANE,)),
            dma((SUBS,)),
            dma((SUBS,)),
            dma((2,)),
            dma((4,)),
            dma((4,)),
            dma((2,)),
            dma((LINE - 1, SUBS)),
            dma((LINE - 1, SUBS)),
            dma((3, SUBS)),
            dma((3, SUBS)),
            dma((SUBS,)),
            pltpu.SemaphoreType.REGULAR,
        ],
        compiler_params=pltpu.CompilerParams(
            collective_id=0, has_side_effects=True, vmem_limit_bytes=60 * 1024 * 1024),
        cost_estimate=pl.CostEstimate(flops=6_500_000_000, bytes_accessed=4_000_000, transcendentals=4_200_000),
    )(latents, codebook)
    quantized, counts_next, codebook_next = pl.pallas_call(
        finish,
        out_shape=(
            jax.ShapeDtypeStruct((ROWS, WIDTH), BF16),
            jax.ShapeDtypeStruct((1, CODES), F32),
            jax.ShapeDtypeStruct((SHARE, CODES), F32),
        ),
        in_specs=[vmem_spec] * 5,
        out_specs=(vmem_spec, vmem_spec, vmem_spec),
        cost_estimate=pl.CostEstimate(flops=300_000, bytes_accessed=2_000_000, transcendentals=0),
    )(quant_t, counts, code_sums, old_counts.reshape(1, CODES), old_sums)
    return quantized, counts_next.reshape(CODES), codebook_next


def solution(mesh):
    return jax.shard_map(
        body,
        mesh=mesh,
        in_specs=(P("dp", None), P("code", None), P("code"), P("dp", "code")),
        out_specs=(P("dp", None), P("code"), P("dp", "code")),
        check_vma=False,
    )
```
